32 devices in a mesh: dp: 2 (over x), seq: 4 (over y, core), wt: 4 (over z).
Axes of the slice: x: 2, y: 2, z: 4, core: 2. Of those that a mesh axis runs over, the one named last changes fastest.
Arguments:
- tokens: bfloat16 [8, 1536, 1536], P(('dp', 'wt'), 'seq'), may hold values from -6 to 6
- cotangent: bfloat16 [8, 1536, 1536], P(('dp', 'wt'), 'seq'), may hold values from -6 to 6
- routes: int32 [8, 1536, 8], P(('dp', 'wt'), 'seq'), may hold values from 0 to 19, all different within a row; in each aligned block of 384 rows (0 to 383, 384 to 767, ..., all dimensions but the last counted through in order) at most 192 rows name the same one
- lengths: int32 [8, 8], P(('dp', 'wt')), may hold values from 1 to 192, 512 in all within a row
- group_adapter_index: int32 [8], P(('dp', 'wt')), may hold values from 0 to 7
- attention_norm_gain: bfloat16 [1536], replicated, may hold values from 0.5 to 1.5
- query_weight: bfloat16 [1536, 1536], P(('dp', 'wt')), may hold values from -0.15625 to 0.15625
- key_value_weight: bfloat16 [1536, 1024], P(('dp', 'wt')), may hold values from -0.15625 to 0.15625
- output_weight: bfloat16 [1536, 1536], P(('dp', 'wt')), may hold values from -1.25 to 1.25
- mixture_norm_gain: bfloat16 [1536], replicated, may hold values from 0.5 to 1.5
- router_weight: bfloat16 [1536, 20], P(('dp', 'wt')), may hold values from -0.078125 to 0.078125
- expert_gate_up_weight: bfloat16 [20, 1536, 1024], P('seq', ('dp', 'wt')), may hold values from -0.15625 to 0.15625
- expert_down_weight: bfloat16 [20, 512, 1536], P('seq', ('dp', 'wt')), may hold values from -0.25 to 0.25
- attention_first_factors: bfloat16 [8, 1536, 48], replicated, may hold values from -0.15625 to 0.15625
- query_second_factor: bfloat16 [8, 16, 1536], replicated, may hold values from -0.75 to 0.75
- key_value_second_factors: bfloat16 [8, 2, 16, 512], replicated, may hold values from -0.75 to 0.75
- output_first_factor: bfloat16 [8, 1536, 16], replicated, may hold values from -1.25 to 1.25
- output_second_factor: bfloat16 [8, 16, 1536], replicated, may hold values from -0.75 to 0.75
- mixture_first_factors: bfloat16 [8, 1536, 48], replicated, may hold values from -0.15625 to 0.15625
- router_second_factor: bfloat16 [8, 16, 20], replicated, may hold values from -0.75 to 0.75
- gate_up_second_factors: bfloat16 [8, 2, 16, 512], replicated, may hold values from -0.75 to 0.75
- down_first_factor: bfloat16 [8, 512, 16], replicated, may hold values from -0.25 to 0.25
- down_second_factor: bfloat16 [8, 16, 1536], replicated, may hold values from -0.75 to 0.75
Outputs:
- output: bfloat16 [8, 1536, 1536], P(('dp', 'wt'), 'seq')
- input_grad: float32 [8, 1536, 1536], P(('dp', 'wt'), 'seq')
- grad_attn_lora_a: float32 [8, 1536, 48], P('wt')
- grad_query_lora_b: float32 [8, 16, 1536], P('wt')
- grad_keyvalue_lora_b: float32 [8, 2, 16, 512], P('wt')
- grad_output_lora_a: float32 [8, 1536, 16], P('wt')
- grad_output_lora_b: float32 [8, 16, 1536], P('wt')
- grad_moe_lora_a: float32 [8, 1536, 48], P('wt')
- grad_router_lora_b: float32 [8, 16, 20], P('wt')
- grad_gate_up_lora_b: float32 [8, 2, 16, 512], P('wt')
- grad_down_lora_a: float32 [8, 512, 16], P('wt')
- grad_down_lora_b: float32 [8, 16, 1536], P('wt')
The draws below stay inside these ranges and needn't reach their ends.
Inputs may be any that keep to these rules, and one draw needn't show every extreme that they name: `routes`: in each aligned block of 384 rows (the rows of one device) no expert is named by more than 192 rows, a bound that some block reaches. `lengths`: each row sums to 512, and its largest entry is 192.
All inputs are finite; a program needn't handle non-finite values.
Results may differ from the reference program's by a relative error of at most 0.018.
Values may be sent and summed in bfloat16 or wider, within the bound.
No kernel may reach another device: no remote copies, remote signals or barrier semaphores. Data moves between devices by JAX's collectives and lax.ppermute only.
A program may use at most 320 MiB of HBM per device.

```python
import math
import jax
import jax.numpy as jnp
import numpy as np
from jax import lax

MODEL_WIDTH = 1536
HEADS = 24
KV_HEADS = 8
HEAD = 64
EXPERT_HIDDEN = 512
TOPK = 8
ADAPTER_RANK = 16
ADAPTER_COUNT = 8
NCONT = 8
EXPERT_COUNT = 20
QUERY_FEATURES = 1536
KEY_FEATURES = 512
PROMPT = 1024
CONT = 512
GROUP_TOK = 1536
TOK_DEV = 384
GROUPS = 8
QBLOCK = 512
CAP = 192
N_SEQ = 4


def set_ends(values, own_key, smallest, largest):
    longest = values.shape.index(max(values.shape))
    spots = []
    for shift in (0, 1):
        where = [jax.random.randint(jax.random.fold_in(own_key, axis), (), 0, length) for axis, length in enumerate(values.shape)]
        where[longest] = (where[longest] + shift) % values.shape[longest]
        spots.append(tuple(where))
    return values.at[spots[0]].set(smallest).at[spots[1]].set(largest)


def block_levels(rng, dims, shards, low, largest):
    loudness, own = 1.0, jax.random.fold_in(rng, 6)
    for dim, parts in shards:
        draws = jnp.exp(jax.random.uniform(jax.random.fold_in(own, dim), (parts,), jnp.float32, low / len(shards), largest / len(shards)))
        loudness = loudness * jnp.repeat(draws, dims[dim] // parts).reshape([-1 if axis == dim else 1 for axis in range(len(dims))])
    return loudness


def profile(amount, total, most, slope):
    weights = [(1 << 20) // math.isqrt(rank ** slope) + 1 for rank in range(2, amount + 1)]
    rest, given = total - most - (amount - 1), [1] * (amount - 1)
    while rest > 0:
        candidates = [i for i in range(amount - 1) if given[i] < most]
        pool, remaining = sum([weights[i] for i in candidates]), rest
        for i in candidates:
            addition = min(most - given[i], max(1, remaining * weights[i] // pool), rest)
            given[i] = given[i] + addition
            rest = rest - addition
    return np.array([most] + given)


def uneven_parts(key, count, total, reach, lean):
    if count == 2:
        one = jax.random.randint(key, (), max(1, total - reach), min(reach, total - 1) + 1)
        return jnp.stack([one, total - one])
    sizes = jnp.asarray(profile(count, total, reach, lean), jnp.int32)
    couples = (count - 1) // 2
    source_of, sink = sizes[1:1 + 2 * couples:2], sizes[2:2 + 2 * couples:2]
    slack = jnp.minimum(source_of - 1, reach - sink)
    moved = jax.random.randint(jax.random.fold_in(key, 1), (couples,), 0, 1 << 20) % (slack + 1)
    sizes = sizes.at[1:1 + 2 * couples:2].set(source_of - moved).at[2:2 + 2 * couples:2].set(sink + moved)
    return sizes[jax.random.permutation(jax.random.fold_in(key, 2), count)]


def deal_out(stream_key, own, number, rows, count, top, limit, lean):
    ranking = jax.random.permutation(stream_key, count)
    heavy_load, ordinary = portions_of(count, rows * top, limit, lean, True), portions_of(count, rows * top, limit, lean, False)
    places = jnp.arange(count)

    def named(sizes, turn):
        used = int((sizes > 0).sum())
        fixed = max(1, used // 4)
        moved = fixed + (places - fixed + turn * (used - fixed)) % max(1, count - fixed)
        return jnp.zeros((count,), jnp.int32).at[ranking[jnp.where(places < fixed, places, moved)]].set(jnp.asarray(sizes, jnp.int32))

    sizes = jnp.where(number % 4 == 0, named(heavy_load, number // 4), named(ordinary, number - number // 4 - 1))
    mixed = jax.random.permutation(jax.random.fold_in(own, 3), count)
    source_of, receiver = mixed[0:count // 2 * 2:2], mixed[1:count // 2 * 2:2]
    margin = jnp.minimum(sizes[source_of] - 1, limit - sizes[receiver]) // 2
    margin = jnp.where((source_of == ranking[0]) | (receiver == ranking[0]) | (sizes[receiver] == 0), 0, jnp.maximum(margin, 0))
    moved = jax.random.randint(jax.random.fold_in(own, 4), (count // 2,), 0, 1 << 20) % (margin + 1)
    sizes = sizes.at[source_of].add(-moved).at[receiver].add(moved)
    members = jnp.searchsorted(jnp.cumsum(sizes), jnp.arange(rows * top), side="right").astype(jnp.int32)
    listing = members.reshape(top, rows).T
    listing = listing[jax.random.permutation(jax.random.fold_in(own, 1), rows)]
    turn = jax.random.randint(jax.random.fold_in(own, 2), (rows, 1), 0, top)
    return jnp.take_along_axis(listing, (jnp.arange(top)[None, :] + turn) % top, axis=1)


def portions_of(amount, total, bound, slope, full):
    portions = [(1 << 20) // math.isqrt(rank ** slope) + 1 for rank in range(1, amount + 1)]
    largest = bound if full else min(bound, max(-(-total // amount), total * portions[0] // sum(portions)))
    least = 1 if total - largest >= amount - 1 else 0
    given, rest = [largest] + [least] * (amount - 1), total - largest - least * (amount - 1)
    while rest > 0:
        free = [i for i in range(1, amount) if given[i] < largest] or [i for i in range(1, amount) if given[i] < bound]
        mass, budget = sum([portions[i] for i in free]), rest
        for i in free:
            addition = min(bound - given[i], max(1, budget * portions[i] // mass), rest)
            given[i] = given[i] + addition
            rest = rest - addition
    return np.array(given)


def scatter_about(stream_key, dims, scale, limit, split=(), kind=jnp.bfloat16):
    entries = jax.random.normal(stream_key, dims, jnp.float32) * scale
    if len(split) > 0:
        entries = block_levels(stream_key, dims, split, -0.22, 0.18) * entries
    return jnp.clip(entries, min=-limit, max=limit).astype(kind)


def setup_inputs(seed: int = 0) -> dict:
    streams_of = jax.random.split(jax.random.key(seed), 24)
    tokens = scatter_about(streams_of[0], (GROUPS, GROUP_TOK, MODEL_WIDTH), 1.0, 6.0, ((0, 8), (1, 4)))
    cotangent = scatter_about(streams_of[1], (GROUPS, GROUP_TOK, MODEL_WIDTH), 1.0, 6.0, ((0, 8), (1, 4)))
    routes_keys = jax.random.split(jax.random.fold_in(streams_of[2], 1), GROUPS * GROUP_TOK // TOK_DEV)
    routes_turns = jax.random.permutation(jax.random.fold_in(streams_of[2], 3), GROUPS * GROUP_TOK // TOK_DEV)
    routes = jax.vmap(lambda own, number: deal_out(jax.random.fold_in(streams_of[2], 2), own, number, TOK_DEV, EXPERT_COUNT, TOPK, CAP, 1))(routes_keys, routes_turns).reshape((GROUPS, GROUP_TOK, TOPK))
    lengths = jax.vmap(lambda own: uneven_parts(own, NCONT, CONT, CONT * 3 // 8, 1))(jax.random.split(streams_of[3], GROUPS)).reshape((GROUPS, NCONT)).astype(jnp.int32)
    group_adapter_index = set_ends(jax.random.randint(streams_of[4], (GROUPS,), 0, ADAPTER_COUNT), jax.random.fold_in(streams_of[4], 1), 0, ADAPTER_COUNT - 1).astype(jnp.int32)
    attention_norm_gain = jnp.clip(1.0 + 0.1 * jax.random.normal(streams_of[5], (MODEL_WIDTH,), jnp.float32), 0.5, 1.5).astype(jnp.bfloat16)
    query_weight = scatter_about(streams_of[6], (MODEL_WIDTH, QUERY_FEATURES), MODEL_WIDTH ** -0.5, 0.15625, ((0, 8),))
    key_value_weight = scatter_about(streams_of[7], (MODEL_WIDTH, 2 * KEY_FEATURES), MODEL_WIDTH ** -0.5, 0.15625, ((0, 8),))
    output_weight = scatter_about(streams_of[8], (QUERY_FEATURES, MODEL_WIDTH), (QUERY_FEATURES // 64) ** -0.5, 1.25, ((0, 8),))
    mixture_norm_gain = jnp.clip(1.0 + 0.1 * jax.random.normal(streams_of[9], (MODEL_WIDTH,), jnp.float32), 0.5, 1.5).astype(jnp.bfloat16)
    router_weight = scatter_about(streams_of[10], (MODEL_WIDTH, EXPERT_COUNT), (4 * MODEL_WIDTH) ** -0.5, 0.078125, ((0, 8),))
    expert_gate_up_weight = scatter_about(streams_of[11], (EXPERT_COUNT, MODEL_WIDTH, 2 * EXPERT_HIDDEN), MODEL_WIDTH ** -0.5, 0.15625, ((0, 4), (1, 8)))
    expert_down_weight = scatter_about(streams_of[12], (EXPERT_COUNT, EXPERT_HIDDEN, MODEL_WIDTH), EXPERT_HIDDEN ** -0.5, 0.25, ((0, 4), (1, 8)))
    attention_first_factors = scatter_about(streams_of[13], (ADAPTER_COUNT, MODEL_WIDTH, 3 * ADAPTER_RANK), MODEL_WIDTH ** -0.5, 0.15625)
    query_second_factor = scatter_about(streams_of[14], (ADAPTER_COUNT, ADAPTER_RANK, QUERY_FEATURES), (4 * ADAPTER_RANK) ** -0.5, 0.75)
    key_value_second_factors = scatter_about(streams_of[15], (ADAPTER_COUNT, 2, ADAPTER_RANK, KEY_FEATURES), (4 * ADAPTER_RANK) ** -0.5, 0.75)
    output_first_factor = scatter_about(streams_of[16], (ADAPTER_COUNT, QUERY_FEATURES, ADAPTER_RANK), (QUERY_FEATURES // 64) ** -0.5, 1.25)
    output_second_factor = scatter_about(streams_of[17], (ADAPTER_COUNT, ADAPTER_RANK, MODEL_WIDTH), (4 * ADAPTER_RANK) ** -0.5, 0.75)
    mixture_first_factors = scatter_about(streams_of[18], (ADAPTER_COUNT, MODEL_WIDTH, 3 * ADAPTER_RANK), MODEL_WIDTH ** -0.5, 0.15625)
    router_second_factor = scatter_about(streams_of[19], (ADAPTER_COUNT, ADAPTER_RANK, EXPERT_COUNT), (4 * ADAPTER_RANK) ** -0.5, 0.75)
    gate_up_second_factors = scatter_about(streams_of[20], (ADAPTER_COUNT, 2, ADAPTER_RANK, EXPERT_HIDDEN), (4 * ADAPTER_RANK) ** -0.5, 0.75)
    down_first_factor = scatter_about(streams_of[21], (ADAPTER_COUNT, EXPERT_HIDDEN, ADAPTER_RANK), EXPERT_HIDDEN ** -0.5, 0.25)
    down_second_factor = scatter_about(streams_of[22], (ADAPTER_COUNT, ADAPTER_RANK, MODEL_WIDTH), (4 * ADAPTER_RANK) ** -0.5, 0.75)
    return dict(tokens=tokens, cotangent=cotangent, routes=routes, lengths=lengths, group_adapter_index=group_adapter_index, attention_norm_gain=attention_norm_gain, query_weight=query_weight, key_value_weight=key_value_weight, output_weight=output_weight, mixture_norm_gain=mixture_norm_gain, router_weight=router_weight, expert_gate_up_weight=expert_gate_up_weight, expert_down_weight=expert_down_weight, attention_first_factors=attention_first_factors, query_second_factor=query_second_factor, key_value_second_factors=key_value_second_factors, output_first_factor=output_first_factor, output_second_factor=output_second_factor, mixture_first_factors=mixture_first_factors, router_second_factor=router_second_factor, gate_up_second_factors=gate_up_second_factors, down_first_factor=down_first_factor, down_second_factor=down_second_factor)


EPS = 1e-05
NEG = -1e+30
PRECISE_MODE = lax.Precision.HIGHEST

@jax.custom_vjp
def reduced_precision(v):
    return lax.optimization_barrier(v.astype(jnp.bfloat16)).astype(jnp.float32)

@jax.custom_vjp
def reduced_precision_back(v):
    return v

def low_keep(v):
    return (reduced_precision(v), None)

def low_pass(kept, grad):
    return (grad,)

def back_keep(v):
    return (v, None)

def back_low(kept, grad):
    return (reduced_precision(grad),)
reduced_precision.defvjp(low_keep, low_pass)
reduced_precision_back.defvjp(back_keep, back_low)

def precise_matmul(left, right):
    return jnp.dot(left, right, precision=PRECISE_MODE)

def rms_norm(value_rows, gain_row):
    return value_rows * lax.rsqrt(lax.optimization_barrier(jnp.mean(value_rows * value_rows, axis=-1, keepdims=True)) + EPS) * gain_row

def layout(lengths_row, prompt_len, total_len):
    ends = jnp.cumsum(lengths_row).astype(jnp.int32)
    starts = (ends - lengths_row).astype(jnp.int32)
    places = jnp.arange(total_len, dtype=jnp.int32)
    offset = (places - prompt_len).astype(jnp.int32)
    counted = lax.optimization_barrier(jnp.sum((offset[:, None] >= ends[None, :]).astype(jnp.int32), axis=1)).astype(jnp.int32)
    inside = offset >= 0
    segment = jnp.where(inside, counted, -1).astype(jnp.int32)
    picked = jnp.arange(lengths_row.shape[0], dtype=jnp.int32)[None, :] == counted[:, None]
    begin = lax.optimization_barrier(jnp.sum(jnp.where(picked, starts[None, :], 0), axis=1)).astype(jnp.int32)
    position = jnp.where(inside, prompt_len + offset - begin, places).astype(jnp.int32)
    return (segment, position)

def rope_tables(position, width):
    half_width = width // 2
    freq = jnp.exp(jnp.arange(half_width, dtype=jnp.float32) * (-2.0 * math.log(10000.0) / width))
    angle = position.astype(jnp.float32)[:, None] * freq[None, :]
    return (jnp.cos(angle), jnp.sin(angle))

def rotate(value_rows, cosine, sine):
    half_width = value_rows.shape[-1] // 2
    first = value_rows[..., :half_width]
    second = value_rows[..., half_width:]
    cos_b = cosine[:, None, :]
    sin_b = sine[:, None, :]
    return jnp.concatenate([first * cos_b - second * sin_b, second * cos_b + first * sin_b], axis=-1)

def forward(hidden_input, adapter_apply, frozen, route, segment, position):
    gain_a, query_matrix, key_value_matrix, output_matrix, gain_m, router_matrix, gate_up_weight_chosen, down_weight_chosen = frozen
    chosen_attention_first, chosen_query_second, chosen_key_value_second, chosen_output_first, chosen_output_second, chosen_mixture_first, chosen_router_second, chosen_gate_up_second, chosen_down_first, chosen_down_second = adapter_apply
    total_len = hidden_input.shape[0]
    attention_normalized = reduced_precision(rms_norm(hidden_input, gain_a))
    attention_rank_state = reduced_precision(precise_matmul(attention_normalized, chosen_attention_first))
    query_rows = precise_matmul(attention_normalized, query_matrix) + precise_matmul(attention_rank_state[:, :ADAPTER_RANK], chosen_query_second)
    key_rows = precise_matmul(attention_normalized, key_value_matrix[:, :KEY_FEATURES]) + precise_matmul(attention_rank_state[:, ADAPTER_RANK:2 * ADAPTER_RANK], chosen_key_value_second[0])
    value_rows = precise_matmul(attention_normalized, key_value_matrix[:, KEY_FEATURES:]) + precise_matmul(attention_rank_state[:, 2 * ADAPTER_RANK:], chosen_key_value_second[1])
    cosine, sine = rope_tables(position, HEAD)
    query_rows = reduced_precision(rotate(reduced_precision_back(query_rows).reshape(total_len, HEADS, HEAD), cosine, sine))
    key_rows = reduced_precision(rotate(reduced_precision_back(key_rows).reshape(total_len, KV_HEADS, HEAD), cosine, sine))
    value_rows = reduced_precision(reduced_precision_back(value_rows)).reshape(total_len, KV_HEADS, HEAD)
    group = HEADS // KV_HEADS
    blocks = total_len // QBLOCK
    q_blocks = query_rows.reshape(blocks, QBLOCK, KV_HEADS, group, HEAD)
    places = jnp.arange(total_len, dtype=jnp.int32)
    scale = HEAD ** (-0.5)

    def attend(group_entry):
        q_block, seg_block, place_block = group_entry
        scores = jnp.einsum('bhgw,thw->hgbt', q_block, key_rows, precision=PRECISE_MODE) * scale
        scores = reduced_precision_back(scores)
        allowed = (places[None, :] <= place_block[:, None]) & ((segment[None, :] < 0) | (segment[None, :] == seg_block[:, None]))
        scores = jnp.where(allowed[None, None], scores, NEG)
        shifted = jnp.exp(scores - lax.optimization_barrier(jnp.max(scores, axis=-1, keepdims=True)))
        probs = shifted / lax.optimization_barrier(jnp.sum(shifted, axis=-1, keepdims=True))
        return jnp.einsum('hgbt,thw->bhgw', reduced_precision(probs), value_rows, precision=PRECISE_MODE)
    attention_output = lax.map(jax.checkpoint(attend), (q_blocks, segment.reshape(blocks, QBLOCK), places.reshape(blocks, QBLOCK)))
    attention_output = reduced_precision(reduced_precision_back(attention_output.reshape(total_len, QUERY_FEATURES)))
    output_rank_state = reduced_precision(precise_matmul(attention_output, chosen_output_first))
    residual_stream = hidden_input + reduced_precision_back(precise_matmul(attention_output, output_matrix) + precise_matmul(output_rank_state, chosen_output_second))
    mixture_normalized = reduced_precision(rms_norm(residual_stream, gain_m))
    mixture_rank_state = reduced_precision(precise_matmul(mixture_normalized, chosen_mixture_first))
    router_logits = precise_matmul(mixture_normalized, router_matrix) + precise_matmul(mixture_rank_state[:, :ADAPTER_RANK], chosen_router_second)
    choose = (route[:, :, None] == jnp.arange(EXPERT_COUNT, dtype=jnp.int32)[None, None, :]).astype(jnp.float32)
    chosen = jnp.einsum('nke,ne->nk', choose, router_logits, precision=PRECISE_MODE)
    gating = jax.nn.softmax(chosen, axis=-1)
    capacity = N_SEQ * CAP
    flat = route.reshape(-1).astype(jnp.int32)
    onehot = (flat[:, None] == jnp.arange(EXPERT_COUNT, dtype=jnp.int32)[None, :]).astype(jnp.int32)
    ranks = lax.optimization_barrier(jnp.sum(onehot * (jnp.cumsum(onehot, axis=0).astype(jnp.int32) - 1), axis=1)).astype(jnp.int32)
    slots = (flat * capacity + ranks).astype(jnp.int32)
    owner_rows = (jnp.arange(flat.shape[0], dtype=jnp.int32) // TOPK).astype(jnp.int32)
    owners = jnp.full((EXPERT_COUNT * capacity,), total_len, jnp.int32).at[slots].set(owner_rows)
    padded = jnp.concatenate([mixture_normalized, jnp.zeros((1, MODEL_WIDTH), mixture_normalized.dtype)], 0)
    padded_z = jnp.concatenate([mixture_rank_state[:, ADAPTER_RANK:], jnp.zeros((1, 2 * ADAPTER_RANK), mixture_rank_state.dtype)], 0)
    token_rows = reduced_precision_back(padded[owners].reshape(EXPERT_COUNT, capacity, MODEL_WIDTH))
    padded_token_rows = reduced_precision_back(padded_z[owners].reshape(EXPERT_COUNT, capacity, 2 * ADAPTER_RANK))
    gate_and_up = jnp.einsum('erd,edf->erf', token_rows, gate_up_weight_chosen, precision=PRECISE_MODE)
    adapter_extra = jnp.concatenate([jnp.einsum('ziw,wy->ziy', padded_token_rows[..., :ADAPTER_RANK], chosen_gate_up_second[0], precision=PRECISE_MODE), jnp.einsum('ziw,wy->ziy', padded_token_rows[..., ADAPTER_RANK:], chosen_gate_up_second[1], precision=PRECISE_MODE)], -1)
    gate_and_up = reduced_precision_back(gate_and_up + adapter_extra)
    expert_activation = reduced_precision(jax.nn.silu(gate_and_up[..., :EXPERT_HIDDEN]) * gate_and_up[..., EXPERT_HIDDEN:])
    down_rank_state = reduced_precision(jnp.einsum('ijm,mn->ijn', expert_activation, chosen_down_first, precision=PRECISE_MODE))
    expert_output = jnp.einsum('umk,ukz->umz', expert_activation, down_weight_chosen, precision=PRECISE_MODE) + jnp.einsum('afp,pv->afv', down_rank_state, chosen_down_second, precision=PRECISE_MODE)
    expert_output = reduced_precision(reduced_precision_back(expert_output))
    picked = expert_output.reshape(EXPERT_COUNT * capacity, MODEL_WIDTH)[slots].reshape(total_len, TOPK, MODEL_WIDTH)
    return residual_stream + jnp.einsum('nk,nkd->nd', gating, picked, precision=PRECISE_MODE)

def reference(tokens, cotangent, routes, lengths, group_adapter_index, attention_norm_gain, query_weight, key_value_weight, output_weight, mixture_norm_gain, router_weight, expert_gate_up_weight, expert_down_weight, attention_first_factors, query_second_factor, key_value_second_factors, output_first_factor, output_second_factor, mixture_first_factors, router_second_factor, gate_up_second_factors, down_first_factor, down_second_factor):
    frozen = tuple((group_entry.astype(jnp.float32) for group_entry in (attention_norm_gain, query_weight, key_value_weight, output_weight, mixture_norm_gain, router_weight, expert_gate_up_weight, expert_down_weight)))
    adapter_banks = tuple((group_entry.astype(jnp.float32) for group_entry in (attention_first_factors, query_second_factor, key_value_second_factors, output_first_factor, output_second_factor, mixture_first_factors, router_second_factor, gate_up_second_factors, down_first_factor, down_second_factor)))

    def one_group(carry, group_entry):
        hidden_input, upstream, route, length_row, index_now = group_entry
        adapter_apply = tuple((lax.dynamic_index_in_dim(bank, index_now, 0, keepdims=False) for bank in adapter_banks))
        segment, position = layout(length_row, PROMPT, GROUP_TOK)

        def run(value_rows, adapters):
            return forward(value_rows, adapters, frozen, route, segment, position)
        result, pull = jax.vjp(run, hidden_input.astype(jnp.float32), adapter_apply)
        grad_in, grad_adapt = pull(upstream.astype(jnp.float32))
        carry = tuple((total_grad.at[index_now].add(grad) for total_grad, grad in zip(carry, grad_adapt)))
        return (carry, (result.astype(jnp.bfloat16), grad_in))
    initial = tuple((jnp.zeros_like(bank) for bank in adapter_banks))
    grads, (outputs, input_grads) = lax.scan(one_group, initial, (tokens, cotangent, routes, lengths, group_adapter_index))
    return (outputs, input_grads, grads[0], grads[1], grads[2], grads[3], grads[4], grads[5], grads[6], grads[7], grads[8], grads[9])
```

```python
import functools
import math

import jax
import jax.numpy as jnp
from jax import lax
from jax.experimental import pallas as pl
from jax.experimental.pallas import tpu as pltpu
from jax.sharding import PartitionSpec as P

MODEL_WIDTH = 1536
HEADS = 24
KV_HEADS = 8
HEAD = 64
HIDDEN = 512
ADAPTER_RANK = 16
ADAPTER_COUNT = 8
PROMPT_LEAST = 1024
PROMPT_DEV = 128
KEY_FEATURES = 512
LANES = 128
SMALL_AT = 96

EPS = 1e-05
NEG = -1e30
F32 = jnp.float32
BF16 = jnp.bfloat16
CHUNKS = (5,)
QB = 256


def dot(a, b, dims=((1,), (0,))):
    return lax.dot_general(a, b, (dims, ((), ())), preferred_element_type=F32)


def dot_nt(a, b):
    return dot(a, b, ((1,), (1,)))


def dot_tn(a, b):
    return dot(a, b, ((0,), (0,)))


def swap_core(x, n_seq):
    return lax.ppermute(x, "seq", [(i, i ^ 1) for i in range(n_seq)])


def shift_chip(x, n_seq, k):
    n_y = n_seq // 2
    pairs = [(y * 2 + c, (y + k) % n_y * 2 + c) for y in range(n_y) for c in range(2)]
    return lax.ppermute(x, "seq", pairs)


def gather_seq(x, n_seq):
    n_y = n_seq // 2
    me = lax.axis_index("seq")
    y, c = me // 2, me % 2
    pieces = [(0, 0, x)]
    far = [shift_chip(x, n_seq, k) for k in range(1, n_y)]
    pieces.append((0, 1, swap_core(x, n_seq)))
    for k, piece in enumerate(far, 1):
        pieces.append((k, 0, piece))
        pieces.append((k, 1, swap_core(piece, n_seq)))
    out = jnp.zeros((n_seq,) + x.shape, x.dtype)
    for k, other, piece in pieces:
        at = (y + n_y - k) % n_y * 2 + (c + other) % 2
        out = lax.dynamic_update_slice_in_dim(out, piece[None], at, 0)
    return out


def scatter_seq(x, n_seq):
    n_y = n_seq // 2
    me = lax.axis_index("seq")
    y, c = me // 2, me % 2

    def block(k, core):
        return lax.dynamic_index_in_dim(x, (y + k) % n_y * 2 + core, 0, keepdims=False)

    total = None
    for k in [*range(1, n_y), 0]:
        got = swap_core(block(k, 1 - c), n_seq)
        both = block(k, c).astype(F32) + got.astype(F32)
        if k:
            both = shift_chip(both.astype(x.dtype), n_seq, k).astype(F32)
        total = both if total is None else total + both
    return total


def shift(x, axis, count, k):
    return lax.ppermute(x, axis, [(i, (i + k) % count) for i in range(count)])


def column_fold(x, op):
    rows, width = x.shape
    return op(x.reshape(rows // 8, 8, width), axis=0)


def attend_kernel(
    prompt_blocks, q_ref, k_ref, v_ref, segq_ref, segk_ref, o_ref, p_ref, inv_ref, krow, scores
):
    i = pl.program_id(1)
    group, qb = q_ref.shape[1], q_ref.shape[3]
    width = group * qb

    @pl.when(i == 0)
    def _():
        krow[...] = k_ref[0].astype(F32).T.astype(BF16)

    q = jnp.concatenate([q_ref[0, h] for h in range(group)], axis=1)
    segq = jnp.concatenate([segq_ref[...]] * group, axis=1)
    placeq = i * qb + lax.broadcasted_iota(jnp.int32, (1, width), 1) % qb

    def score(j, peak, masked):
        rows = pl.ds(pl.multiple_of(j * qb, qb), qb)
        s = dot(krow[rows, :], q)
        if masked:
            segk = segk_ref[rows, :]
            placek = j * qb + lax.broadcasted_iota(jnp.int32, (qb, 1), 0)
            keep = (placek <= placeq) & ((segk < 0) | (segk == segq))
            s = jnp.where(keep, s, NEG)
        scores[rows, :] = s
        return jnp.maximum(peak, column_fold(s, jnp.max))

    free = jnp.minimum(i, prompt_blocks)
    peak = jnp.full((8, width), NEG, F32)
    peak = lax.fori_loop(0, free, lambda j, m: score(j, m, False), peak)
    peak = lax.fori_loop(free, i + 1, lambda j, m: score(j, m, True), peak)
    peak = jnp.max(peak, axis=0, keepdims=True)

    def weigh(j, carry):
        total, acc = carry
        rows = pl.ds(pl.multiple_of(j * qb, qb), qb)
        p = jnp.exp(scores[rows, :] - peak)
        low = p.astype(BF16)
        p_ref[0, 0, rows, :] = low
        return total + column_fold(p, jnp.sum), acc + dot(v_ref[0, :, rows], low)

    total, acc = lax.fori_loop(
        0, i + 1, weigh, (jnp.zeros((8, width), F32), jnp.zeros((HEAD, width), F32))
    )
    inverse = 1.0 / jnp.sum(total, axis=0, keepdims=True)
    inv_ref[0, 0] = inverse
    out = (acc * inverse).astype(BF16)
    for h in range(group):
        o_ref[0, h] = out[:, h * qb : (h + 1) * qb]


def attend(qt, kt, vt, segment, prompt_len):
    kv, group, _, total = qt.shape
    blocks = total // QB
    width = group * QB
    pairs = kv * group * total * total // 2
    return pl.pallas_call(
        functools.partial(attend_kernel, prompt_len // QB),
        grid=(kv, blocks),
        in_specs=[
            pl.BlockSpec((1, group, HEAD, QB), lambda b, i: (b, 0, 0, i)),
            pl.BlockSpec((1, HEAD, total), lambda b, i: (b, 0, 0)),
            pl.BlockSpec((1, HEAD, total), lambda b, i: (b, 0, 0)),
            pl.BlockSpec((1, QB), lambda b, i: (0, i)),
            pl.BlockSpec((total, 1), lambda b, i: (0, 0)),
        ],
        out_specs=[
            pl.BlockSpec((1, group, HEAD, QB), lambda b, i: (b, 0, 0, i)),
            pl.BlockSpec((1, 1, total, width), lambda b, i: (b, i, 0, 0)),
            pl.BlockSpec((1, 1, 1, width), lambda b, i: (b, i, 0, 0)),
        ],
        out_shape=[
            jax.ShapeDtypeStruct(qt.shape, BF16),
            jax.ShapeDtypeStruct((kv, blocks, total, width), BF16),
            jax.ShapeDtypeStruct((kv, blocks, 1, width), F32),
        ],
        scratch_shapes=[pltpu.VMEM((total, HEAD), BF16), pltpu.VMEM((total, width), F32)],
        compiler_params=pltpu.CompilerParams(vmem_limit_bytes=40 * 2**20),
        cost_estimate=pl.CostEstimate(
            flops=pairs * HEAD * 4, bytes_accessed=pairs * 4, transcendentals=pairs
        ),
    )(qt, kt, vt, segment[None, :], segment[:, None])


def unrotate(grad, cosine, sine):
    half = HEAD // 2
    first, second = grad[:half], grad[half:]
    return jnp.concatenate(
        [first * cosine + second * sine, second * cosine - first * sine], axis=0
    )


def attend_back_kernel(
    q_ref, k_ref, v_ref, o_ref, do_ref, p_ref, inv_ref, cosq_ref, sinq_ref, cos_ref, sin_ref,
    dq_ref, dk_ref, dv_ref, vrow, dk_acc, dv_acc,
):
    i = pl.program_id(1)
    group, qb = q_ref.shape[1], q_ref.shape[3]
    width = group * qb

    @pl.when(i == 0)
    def _():
        vrow[...] = v_ref[0].astype(F32).T.astype(BF16)
        dk_acc[...] = jnp.zeros_like(dk_acc)
        dv_acc[...] = jnp.zeros_like(dv_acc)

    def side(ref):
        return jnp.concatenate([ref[0, h].astype(F32) for h in range(group)], axis=1)

    do = side(do_ref) * inv_ref[0, 0]
    centre = jnp.sum(side(o_ref) * do, axis=0, keepdims=True)
    do_low = do.astype(BF16)
    do_rows = do.T.astype(BF16)
    q_rows = side(q_ref).T.astype(BF16)

    def step(j, acc):
        rows = pl.ds(pl.multiple_of(j * qb, qb), qb)
        p = p_ref[0, 0, rows, :]
        dp = dot(vrow[rows, :], do_low)
        ds = (p.astype(F32) * (dp - centre)).astype(BF16)
        dk_acc[rows, :] += dot(ds, q_rows)
        dv_acc[rows, :] += dot(p, do_rows)
        return acc + dot(k_ref[0, :, rows], ds)

    dq = lax.fori_loop(0, i + 1, step, jnp.zeros((HEAD, width), F32)) * HEAD**-0.5
    for h in range(group):
        part = dq[:, h * qb : (h + 1) * qb]
        dq_ref[0, h] = unrotate(part, cosq_ref[...], sinq_ref[...]).astype(BF16)

    @pl.when(i == pl.num_programs(1) - 1)
    def _():
        dk_ref[0] = unrotate(dk_acc[...].T, cos_ref[...], sin_ref[...]).astype(BF16)
        dv_ref[0] = dv_acc[...].T.astype(BF16)


def attend_back(qt, kt, vt, ot, dot_, p, inverse, cosine, sine):
    kv, group, _, total = qt.shape
    blocks = total // QB
    width = group * QB
    pairs = kv * group * total * total // 2
    q_spec = pl.BlockSpec((1, group, HEAD, QB), lambda b, i: (b, 0, 0, i))
    k_spec = pl.BlockSpec((1, HEAD, total), lambda b, i: (b, 0, 0))
    return pl.pallas_call(
        attend_back_kernel,
        grid=(kv, blocks),
        in_specs=[
            q_spec, k_spec, k_spec, q_spec, q_spec,
            pl.BlockSpec((1, 1, total, width), lambda b, i: (b, i, 0, 0)),
            pl.BlockSpec((1, 1, 1, width), lambda b, i: (b, i, 0, 0)),
            pl.BlockSpec((HEAD // 2, QB), lambda b, i: (0, i)),
            pl.BlockSpec((HEAD // 2, QB), lambda b, i: (0, i)),
            pl.BlockSpec((HEAD // 2, total), lambda b, i: (0, 0)),
            pl.BlockSpec((HEAD // 2, total), lambda b, i: (0, 0)),
        ],
        out_specs=[q_spec, k_spec, k_spec],
        out_shape=[
            jax.ShapeDtypeStruct(qt.shape, BF16),
            jax.ShapeDtypeStruct(kt.shape, BF16),
            jax.ShapeDtypeStruct(vt.shape, BF16),
        ],
        scratch_shapes=[
            pltpu.VMEM((total, HEAD), BF16),
            pltpu.VMEM((total, HEAD), F32),
            pltpu.VMEM((total, HEAD), F32),
        ],
        compiler_params=pltpu.CompilerParams(vmem_limit_bytes=40 * 2**20),
        cost_estimate=pl.CostEstimate(
            flops=pairs * HEAD * 8, bytes_accessed=pairs * 4, transcendentals=0
        ),
    )(qt, kt, vt, ot, dot_, p, inverse, cosine, sine, cosine, sine)


def pack_experts(gate_up, down):
    parts = [gate_up[..., :HIDDEN], gate_up[..., HIDDEN:]]
    parts += [down[..., m : m + HIDDEN] for m in range(0, MODEL_WIDTH, HIDDEN)]
    return jnp.concatenate(parts, axis=1)


def expert_kernel(
    first, last, shards_count, rows, hidden_rows, experts_all, place_ref, x_ref, dy_ref, gate_ref,
    small_ref, s_ref, gus_ref, dfat_ref, dfa_ref, dsf_ref, back_ref, *refs,
):
    refs = list(refs)
    carried = [] if first else [refs.pop(0) for _ in range(5)]
    shards = [refs.pop(0) for _ in range(shards_count)]
    outs = [refs.pop(0) for _ in range(5)]
    w_up, w_down, zbias, sbias, out_acc, row_acc, aux_acc, wi_acc, db_acc, sem = refs
    count = w_up.shape[0]
    tile = x_ref.shape[0]
    accs = (out_acc, row_acc, aux_acc, wi_acc, db_acc)

    @pl.when(pl.program_id(0) == 0)
    def _():
        copies = []
        for b, shard in enumerate(shards):
            index = place_ref[1 + b]
            up_rows = pl.ds(pl.multiple_of(index * rows, rows), rows)
            down_rows = pl.ds(pl.multiple_of(index * hidden_rows, hidden_rows), hidden_rows)
            for m in range(2):
                copies.append((shard.at[:, pl.ds(m * rows, rows), :],
                               w_up.at[:, up_rows, pl.ds(m * HIDDEN, HIDDEN)]))
            for m in range(MODEL_WIDTH // HIDDEN):
                copies.append((shard.at[:, pl.ds(2 * rows + m * hidden_rows, hidden_rows), :],
                               w_down.at[:, down_rows, pl.ds(m * HIDDEN, HIDDEN)]))
        copies = [pltpu.make_async_copy(a, b, sem.at[n]) for n, (a, b) in enumerate(copies)]
        for copy in copies:
            copy.start()
        for copy in copies:
            copy.wait()

    for n, acc in enumerate(accs):
        acc[...] = jnp.zeros_like(acc) if first else carried[n][...]
    zbias[...] = dot(small_ref[...], gus_ref[...])
    sbias[...] = dot(s_ref[...], dfat_ref[...])
    lane = lax.broadcasted_iota(jnp.int32, (tile, LANES), 1)

    def step(e, _):
        name = place_ref[0] + e
        x, dy = x_ref[...], dy_ref[...]
        both = dot(x, w_up[e]) + zbias[...]
        gate_in, up = both[:, :HIDDEN], both[:, HIDDEN:]
        sigma = jax.nn.sigmoid(gate_in)
        silu = gate_in * sigma
        inner = silu * up
        d_down = dot_nt(dy, w_down[e]) + sbias[...]
        d_gating = jnp.sum(inner * d_down, axis=1, keepdims=True)
        gating = jnp.sum(jnp.where(lane == name, gate_ref[...], 0.0), axis=1, keepdims=True)
        aux_acc[...] += jnp.where((lane == name) | (lane == name + experts_all), d_gating, 0.0)
        gated = gating * inner
        wi_acc[...] += gated
        out_acc[...] += dot(gated.astype(BF16), w_down[e])
        d_inner = gating * d_down
        d_gate = d_inner * up * sigma * (1.0 + gate_in * (1.0 - sigma))
        d_both = jnp.concatenate([d_gate, d_inner * silu], axis=1)
        db_acc[...] += d_both
        row_acc[...] += dot_nt(d_both.astype(BF16), w_up[e])
        return 0

    lax.fori_loop(0, count, step, 0)
    if not last:
        for out, acc in zip(outs, accs):
            out[...] = acc[...]
        return
    low_wi, low_db = wi_acc[...].astype(BF16), db_acc[...].astype(BF16)
    small_d = dot(low_wi, dfa_ref[...]).astype(BF16)
    outs[0][...] = (out_acc[...] + dot(small_d, dsf_ref[...])).astype(BF16)
    aux = aux_acc[...] + dot(low_db, back_ref[...])
    high = aux.astype(BF16)
    rest = (aux - high.astype(F32)).astype(BF16)
    is_rest = (lane >= experts_all) & (lane < 2 * experts_all)
    outs[1][:, :MODEL_WIDTH] = row_acc[...].astype(BF16)
    outs[1][:, MODEL_WIDTH:] = jnp.where(is_rest, rest, high)
    outs[2][...] = small_d
    outs[3][...] = low_wi
    outs[4][...] = low_db


def run_experts(place, x, dy, gates, small, s, mats, carried, shards, experts_all, last, tile):
    total = x.shape[0]
    count, packed_rows, _ = shards[0].shape
    rows = MODEL_WIDTH // len(shards)
    hidden_rows = HIDDEN // len(shards)
    first = carried is None
    widths = (MODEL_WIDTH, MODEL_WIDTH + LANES if last else MODEL_WIDTH, LANES, HIDDEN, 2 * HIDDEN)
    dtype = BF16 if last else F32

    def tiled(width):
        return pl.BlockSpec((tile, width), lambda t, _: (t, 0))

    def whole(shape):
        return pl.BlockSpec(shape, lambda t, _: (0, 0))

    in_widths = (MODEL_WIDTH, MODEL_WIDTH, LANES, LANES, LANES)
    acc_widths = (MODEL_WIDTH, MODEL_WIDTH, LANES, HIDDEN, 2 * HIDDEN)
    specs = [tiled(w) for w in in_widths] + [whole(m.shape) for m in mats]
    specs += [] if first else [tiled(w) for w in acc_widths]
    specs += [pl.BlockSpec(memory_space=pl.ANY)] * len(shards)
    copies = len(shards) * (2 + MODEL_WIDTH // HIDDEN)
    return pl.pallas_call(
        functools.partial(
            expert_kernel, first, last, len(shards), rows, hidden_rows, experts_all
        ),
        grid_spec=pltpu.PrefetchScalarGridSpec(
            num_scalar_prefetch=1,
            grid=(total // tile,),
            in_specs=specs,
            out_specs=[tiled(w) for w in widths],
            scratch_shapes=[
                pltpu.VMEM((count, MODEL_WIDTH, 2 * HIDDEN), BF16),
                pltpu.VMEM((count, HIDDEN, MODEL_WIDTH), BF16),
                pltpu.VMEM((tile, 2 * HIDDEN), F32),
                pltpu.VMEM((tile, HIDDEN), F32),
                *[pltpu.VMEM((tile, w), F32) for w in acc_widths],
                pltpu.SemaphoreType.DMA((copies,)),
            ],
        ),
        out_shape=[jax.ShapeDtypeStruct((total, w), dtype) for w in widths],
        compiler_params=pltpu.CompilerParams(vmem_limit_bytes=60 * 2**20),
        cost_estimate=pl.CostEstimate(
            flops=12 * total * MODEL_WIDTH * HIDDEN * count,
            bytes_accessed=total * MODEL_WIDTH * 10,
            transcendentals=total * HIDDEN * count,
        ),
    )(place, x, dy, gates, small, s, *mats, *(carried or ()), *shards)


def norm_backward(value_rows, inverse, gain_row, upstream):
    scaled = upstream * gain_row
    inner_mean = jnp.mean(value_rows * scaled, axis=-1, keepdims=True)
    return inverse * scaled - value_rows * (inverse * inverse * inverse) * inner_mean


def layout(lengths_row, prompt_len, total_len):
    ends = jnp.sum(jnp.tril(jnp.ones((lengths_row.shape[0],) * 2, jnp.int32)) * lengths_row, axis=1)
    starts = ends - lengths_row
    places = jnp.arange(total_len, dtype=jnp.int32)
    offset = places - prompt_len
    counted = jnp.sum((offset[:, None] >= ends[None, :]).astype(jnp.int32), axis=1)
    inside = offset >= 0
    segment = jnp.where(inside, counted, -1)
    picked = jnp.arange(lengths_row.shape[0], dtype=jnp.int32)[None, :] == counted[:, None]
    begin = jnp.sum(jnp.where(picked, starts[None, :], 0), axis=1)
    position = jnp.where(inside, prompt_len + offset - begin, places)
    return (segment, position)


def pad_lanes(x, at=0, width=LANES):
    return jnp.pad(x, ((0, 0), (at, width - at - x.shape[1])))


def stack_rows(grads):
    rows = []
    for grad in grads:
        for m in range(0, grad.shape[1], HIDDEN):
            rows.append(grad[:, m : m + HIDDEN])
    return jnp.concatenate(rows, axis=0)


def unstack_rows(flat, shapes):
    out, at = [], 0
    for height, width in shapes:
        parts = []
        for _ in range(width // HIDDEN):
            parts.append(flat[:, at : at + height])
            at += height
        out.append(jnp.concatenate(parts, axis=2) if len(parts) > 1 else parts[0])
    return out


def reduce_adapters(flat, n_seq, n_dp, n_wt, index_now):
    rows = flat.shape[0]
    mine = scatter_seq(flat.reshape(n_seq, rows // n_seq, HIDDEN), n_seq)
    tag = jnp.full((8, HIDDEN), index_now.astype(F32))
    everyone = lax.all_gather(jnp.concatenate([mine, tag], 0), ("dp", "wt"), axis=0)
    share = ADAPTER_COUNT // n_wt
    first_row = lax.axis_index("wt") * share
    names = everyone[:, -1, 0].astype(jnp.int32)
    picks = (names[None, :] == first_row + jnp.arange(share)[:, None]).astype(F32)
    kept = jnp.sum(picks[:, :, None, None] * everyone[None, :, :-8], axis=1)
    full = gather_seq(kept.reshape(share * (rows // n_seq), HIDDEN), n_seq)
    full = full.reshape(n_seq, share, rows // n_seq, HIDDEN)
    return jnp.swapaxes(full, 0, 1).reshape(share, rows, HIDDEN)


def shards(
    tokens,
    cotangent,
    routes,
    lengths,
    group_adapter_index,
    attention_norm_gain,
    query_weight,
    key_value_weight,
    output_weight,
    mixture_norm_gain,
    router_weight,
    expert_gate_up_weight,
    expert_down_weight,
    attention_first_factors,
    query_second_factor,
    key_value_second_factors,
    output_first_factor,
    output_second_factor,
    mixture_first_factors,
    router_second_factor,
    gate_up_second_factors,
    down_first_factor,
    down_second_factor,
):
    n_seq, n_dp, n_wt = (lax.axis_size(a) for a in ("seq", "dp", "wt"))
    seq, dp, wt = (lax.axis_index(a) for a in ("seq", "dp", "wt"))
    local = tokens.shape[1]
    total = local * n_seq
    prompt_len = max(PROMPT_LEAST, PROMPT_DEV * n_seq)
    exp_dev = expert_gate_up_weight.shape[0]
    experts_all = exp_dev * n_seq
    kv_local = KV_HEADS // n_seq
    group = HEADS // KV_HEADS
    q_width = MODEL_WIDTH // n_seq
    k_width = KEY_FEATURES // n_seq
    rank = ADAPTER_RANK
    index_now = group_adapter_index[0]

    def chosen(bank):
        return lax.dynamic_index_in_dim(bank, index_now, 0, keepdims=False)

    def own(x, size, axis=1, at=0):
        return lax.dynamic_slice_in_dim(x, at + seq * size, size, axis)

    attn_first = chosen(attention_first_factors)
    query_second = own(chosen(query_second_factor), q_width)
    kv_second = chosen(key_value_second_factors)
    out_first = chosen(output_first_factor)
    out_second = chosen(output_second_factor)
    mix_first = chosen(mixture_first_factors)
    router_second = chosen(router_second_factor)
    gate_up_second = chosen(gate_up_second_factors)
    down_first = chosen(down_first_factor)
    down_second = chosen(down_second_factor)

    bounds = [0]
    for size in CHUNKS:
        bounds.append(bounds[-1] + size)
    expert_shards = []
    for lo, hi in zip(bounds[:-1], bounds[1:]):
        packed = pack_experts(expert_gate_up_weight[lo:hi], expert_down_weight[lo:hi])
        column = [packed]
        for _ in range(1, n_wt):
            column.append(shift(column[-1], "wt", n_wt, 1))
        pieces = []
        for k in range(n_dp):
            pieces += [(k, b, shift(x, "dp", n_dp, k) if k else x) for b, x in enumerate(column)]
        expert_shards.append(pieces)
    order = [
        (dp + n_dp - k) % n_dp * n_wt + (wt + n_wt - b) % n_wt for k, b, _ in expert_shards[0]
    ]

    hidden = gather_seq(tokens[0], n_seq).reshape(total, MODEL_WIDTH)
    named = jnp.arange(LANES, dtype=jnp.int32)[None, None, :]
    mask = jnp.any(routes[0][:, :, None] == named, axis=1).astype(BF16)
    upstream_all = gather_seq(jnp.concatenate([cotangent[0], mask], axis=1), n_seq)
    upstream_all = upstream_all.reshape(total, MODEL_WIDTH + LANES)
    d_out_all = upstream_all[:, :MODEL_WIDTH]
    routed = upstream_all[:, MODEL_WIDTH : MODEL_WIDTH + experts_all] > 0.5

    mine = jnp.concatenate(
        [
            own(query_weight, q_width),
            own(key_value_weight, k_width),
            own(key_value_weight, k_width, at=KEY_FEATURES),
            pad_lanes(router_weight),
        ],
        axis=1,
    )
    gathered = lax.all_gather(mine, ("dp", "wt"), axis=0, tiled=True)
    qkv_width = q_width + 2 * k_width
    qkv_weight = gathered[:, :qkv_width]
    router_full = gathered[:, qkv_width : qkv_width + experts_all]
    half = MODEL_WIDTH // 2
    core = seq % 2
    out_mine = lax.all_gather(
        lax.dynamic_slice_in_dim(output_weight, core * half, half, 1), ("dp", "wt"), axis=0, tiled=True
    )
    out_other = swap_core(out_mine, n_seq)
    out_weight = jnp.where(
        core == 0,
        jnp.concatenate([out_mine, out_other], 1),
        jnp.concatenate([out_other, out_mine], 1),
    )

    gain_first = attention_norm_gain.astype(F32)
    gain_second = mixture_norm_gain.astype(F32)
    hidden_f = hidden.astype(F32)
    inverse_a = lax.rsqrt(jnp.mean(hidden_f * hidden_f, axis=-1, keepdims=True) + EPS)
    normed = (hidden_f * inverse_a * gain_first).astype(BF16)
    small_a = dot(normed, attn_first).astype(BF16)
    second = jnp.zeros((3 * rank, qkv_width), BF16)
    second = second.at[:rank, :q_width].set(query_second)
    second = second.at[rank : 2 * rank, q_width : q_width + k_width].set(own(kv_second[0], k_width))
    second = second.at[2 * rank :, q_width + k_width :].set(own(kv_second[1], k_width))
    qkv = dot(qkv_weight, normed, ((0,), (1,))) + dot(second, small_a, ((0,), (1,)))
    segment, position = layout(lengths[0], prompt_len, total)
    freq = jnp.exp(jnp.arange(HEAD // 2, dtype=F32) * (-2.0 * math.log(10000.0) / HEAD))
    angle = freq[:, None] * position.astype(F32)[None, :]
    cosine, sine = jnp.cos(angle), jnp.sin(angle)

    def rotate(x, scale=1.0):
        x = x.reshape(-1, 2, HEAD // 2, total)
        a, b = x[:, 0], x[:, 1]
        x = jnp.concatenate([a * cosine - b * sine, b * cosine + a * sine], axis=1)
        return (x.astype(BF16) * jnp.asarray(scale, BF16)).reshape(-1, HEAD, total)

    qt = rotate(qkv[:q_width], HEAD**-0.5).reshape(kv_local, group, HEAD, total)
    kt = rotate(qkv[q_width : q_width + k_width])
    vt = qkv[q_width + k_width :].astype(BF16).reshape(kv_local, HEAD, total)
    ot, probs, inverse_l = attend(qt, kt, vt, segment, prompt_len)
    att = gather_seq(ot.reshape(q_width, total), n_seq).reshape(MODEL_WIDTH, total)

    small_o = dot_tn(att, out_first).astype(BF16)
    residual = hidden_f + dot_tn(att, out_weight) + dot(small_o, out_second)
    inverse_m = lax.rsqrt(jnp.mean(residual * residual, axis=-1, keepdims=True) + EPS)
    normed_m = (residual * inverse_m * gain_second).astype(BF16)
    mix_router = jnp.concatenate([mix_first, router_full], axis=1)
    states = dot(normed_m, mix_router)
    small_m = states[:, : 3 * rank].astype(BF16)
    logits = states[:, 3 * rank :] + dot(small_m[:, :rank], router_second)
    logits = jnp.where(routed, logits, NEG)
    peak = jnp.max(logits, axis=-1, keepdims=True)
    weights = jnp.where(routed, jnp.exp(logits - peak), 0.0)
    gating = weights / jnp.sum(weights, axis=-1, keepdims=True)

    d_rank = dot_nt(d_out_all, down_second).astype(BF16)
    gus = jnp.zeros((LANES, 2 * HIDDEN), BF16)
    gus = gus.at[:rank, :HIDDEN].set(gate_up_second[0])
    gus = gus.at[rank : 2 * rank, HIDDEN:].set(gate_up_second[1])
    back = jnp.zeros((2 * HIDDEN, LANES), BF16)
    back = back.at[:, SMALL_AT : SMALL_AT + 2 * rank].set(gus[: 2 * rank].T)
    mats = (
        gus,
        jnp.pad(down_first.T, ((0, LANES - rank), (0, 0))),
        pad_lanes(down_first),
        jnp.pad(down_second, ((0, LANES - rank), (0, 0))),
        back,
    )
    gates = pad_lanes(gating)
    small_pad = pad_lanes(small_m[:, rank:])
    rank_pad = pad_lanes(d_rank)
    carried = None
    for n, pieces in enumerate(expert_shards):
        place = jnp.stack([(seq * exp_dev + bounds[n]).astype(jnp.int32)] + order)
        carried = run_experts(
            place.astype(jnp.int32), normed_m, d_out_all, gates, small_pad, rank_pad, mats, carried,
            [x for _, _, x in pieces], experts_all, n == len(expert_shards) - 1, 256,
        )
    part_out, part_back, small_d, weighted_inner, d_both = carried
    small_d = small_d[:, :rank]

    def own_rows(x):
        return lax.dynamic_slice_in_dim(x, seq * local, local, 0)

    back_sum = scatter_seq(part_back.reshape(n_seq, local, MODEL_WIDTH + LANES), n_seq)
    upstream = cotangent[0].astype(F32)
    residual_own = own_rows(residual)
    gating_own = own_rows(gating)
    small_m_own = own_rows(small_m)
    d_gating = (
        back_sum[:, MODEL_WIDTH : MODEL_WIDTH + experts_all]
        + back_sum[:, MODEL_WIDTH + experts_all : MODEL_WIDTH + 2 * experts_all]
    )
    d_logits = gating_own * (d_gating - jnp.sum(d_gating * gating_own, axis=-1, keepdims=True))
    d_logits_low = d_logits.astype(BF16)
    d_small_m = jnp.concatenate(
        [dot_nt(d_logits_low, router_second), back_sum[:, MODEL_WIDTH + SMALL_AT :]], axis=1
    ).astype(BF16)
    d_normed_m = back_sum[:, :MODEL_WIDTH] + dot_nt(
        jnp.concatenate([d_small_m, d_logits_low], axis=1), mix_router
    )
    d_residual = upstream + norm_backward(
        residual_own, own_rows(inverse_m), gain_second, d_normed_m
    )
    d_branch = d_residual.astype(BF16)
    d_small_o = dot_nt(d_branch, out_second).astype(BF16)
    d_att = (dot_nt(out_weight, d_branch) + dot_nt(out_first, d_small_o)).astype(BF16)
    d_att = lax.all_to_all(d_att, "seq", split_axis=0, concat_axis=1, tiled=True)
    dqt, dkt, dvt = attend_back(
        qt, kt, vt, ot, d_att.reshape(kv_local, group, HEAD, total), probs, inverse_l, cosine, sine
    )
    d_qkv = jnp.concatenate(
        [dqt.reshape(q_width, total), dkt.reshape(k_width, total), dvt.reshape(k_width, total)], 0
    )
    d_small_a = dot(d_qkv, second, ((0,), (1,))).astype(BF16)
    d_normed = dot(d_qkv, qkv_weight, ((0,), (1,))) + dot_nt(d_small_a, attn_first)
    d_normed = scatter_seq(d_normed.astype(BF16).reshape(n_seq, local, MODEL_WIDTH), n_seq)
    input_grad = d_residual + norm_backward(
        tokens[0].astype(F32), own_rows(inverse_a), gain_first, d_normed
    )
    output_rows = residual_own + scatter_seq(part_out.reshape(n_seq, local, MODEL_WIDTH), n_seq)

    grad_second = dot(small_a, d_qkv, ((0,), (1,)))

    def spread(x, width, full):
        return lax.dynamic_update_slice_in_dim(
            jnp.zeros((x.shape[0], full), F32), x, seq * width, 1
        )

    grad_q_b = spread(grad_second[:rank, :q_width], q_width, MODEL_WIDTH)
    grad_k_b = spread(grad_second[rank : 2 * rank, q_width : q_width + k_width], k_width, KEY_FEATURES)
    grad_v_b = spread(grad_second[2 * rank :, q_width + k_width :], k_width, KEY_FEATURES)
    grad_gu = dot_tn(small_m[:, rank:], d_both)
    att_own = lax.dynamic_slice_in_dim(att, seq * local, local, 1)
    grads = [
        dot_tn(d_small_a, normed),
        grad_q_b,
        grad_k_b,
        grad_v_b,
        dot(d_small_o, att_own, ((0,), (1,))),
        dot_tn(own_rows(small_o), d_branch),
        dot_tn(d_small_m, own_rows(normed_m)),
        pad_lanes(dot_tn(small_m_own[:, :rank], d_logits_low), width=HIDDEN),
        grad_gu[:rank, :HIDDEN],
        grad_gu[rank:, HIDDEN:],
        dot_tn(d_rank, weighted_inner),
        dot_tn(small_d, d_out_all),
    ]
    flat = reduce_adapters(stack_rows(grads), n_seq, n_dp, n_wt, index_now)
    attn_a, q_b, k_b, v_b, o_a, o_b, moe_a, r_b, gate_b, up_b, down_a, down_b = unstack_rows(
        flat, [g.shape for g in grads]
    )

    def flip(x):
        return jnp.swapaxes(x, 1, 2)

    return (
        output_rows[None].astype(BF16),
        input_grad[None],
        flip(attn_a),
        q_b,
        jnp.stack([k_b, v_b], axis=1),
        flip(o_a),
        o_b,
        flip(moe_a),
        r_b[:, :, :experts_all],
        jnp.stack([gate_b, up_b], axis=1),
        flip(down_a),
        down_b,
    )


def solution(mesh):
    split = P(("dp", "wt"), "seq", None)
    rows = P(("dp", "wt"), None)
    bank = P("wt", None, None)
    placed = (
        split, split, split, rows, P(("dp", "wt")), P(), rows, rows, rows, P(), rows,
        P("seq", ("dp", "wt"), None), P("seq", ("dp", "wt"), None),
    ) + (P(),) * 10
    wide = P("wt", None, None, None)
    return jax.shard_map(
        shards,
        mesh=mesh,
        in_specs=placed,
        out_specs=(split, split, bank, bank, wide, bank, bank, bank, bank, wide, bank, bank),
        check_vma=False,
    )
```

```python
import functools
import math

import jax
import jax.numpy as jnp
from jax import lax
from jax.experimental import pallas as pl
from jax.experimental.pallas import tpu as pltpu
from jax.sharding import PartitionSpec as P

MODEL_WIDTH = 1536
HEADS = 24
KV_HEADS = 8
HEAD = 64
HIDDEN = 512
ADAPTER_RANK = 16
ADAPTER_COUNT = 8
PROMPT_LEAST = 1024
PROMPT_DEV = 128
KEY_FEATURES = 512
LANES = 128
SMALL_AT = 96

EPS = 1e-05
NEG = -1e30
F32 = jnp.float32
BF16 = jnp.bfloat16
FIRST_EXPERTS = 3
TILE = 256
DOWN_AT = 80


def dot(a, b, dims=((1,), (0,))):
    return lax.dot_general(a, b, (dims, ((), ())), preferred_element_type=F32)


def dot_nt(a, b):
    return dot(a, b, ((1,), (1,)))


def dot_tn(a, b):
    return dot(a, b, ((0,), (0,)))


def swap_core(x, n_seq):
    return lax.ppermute(x, "seq", [(i, i ^ 1) for i in range(n_seq)])


def shift_chip(x, n_seq, k):
    n_y = n_seq // 2
    pairs = [(y * 2 + c, (y + k) % n_y * 2 + c) for y in range(n_y) for c in range(2)]
    return lax.ppermute(x, "seq", pairs)


def seq_pieces(x, n_seq):
    n_y = n_seq // 2
    me = lax.axis_index("seq")
    y, c = me // 2, me % 2
    far = [shift_chip(x, n_seq, k) for k in range(1, n_y)]
    pieces = [(me, x), (me ^ 1, swap_core(x, n_seq))]
    for k, piece in enumerate(far, 1):
        chip = (y + n_y - k) % n_y * 2
        pieces += [(chip + c, piece), (chip + 1 - c, swap_core(piece, n_seq))]
    return pieces


def gather_seq(x, n_seq):
    out = jnp.zeros((n_seq,) + x.shape, x.dtype)
    for at, piece in seq_pieces(x, n_seq):
        out = lax.dynamic_update_slice_in_dim(out, piece[None], at, 0)
    return out


def core_sum(x, n_seq):
    c = lax.axis_index("seq") % 2
    got = swap_core(lax.dynamic_index_in_dim(x, 1 - c, 0, keepdims=False), n_seq)
    kept = lax.dynamic_index_in_dim(x, c, 0, keepdims=False)
    return kept.astype(F32) + got.astype(F32)


def scatter_piece(x, n_seq, k):
    both = core_sum(x, n_seq)
    return shift_chip(both.astype(x.dtype), n_seq, k).astype(F32) if k else both


def chip_turns(n_seq):
    n_y = n_seq // 2
    y = lax.axis_index("seq") // 2
    return [(k, (y + k) % n_y) for k in [*range(1, n_y), 0]]


def scatter_seq(x, n_seq):
    x = x.reshape((n_seq // 2, 2) + x.shape[1:])
    return sum(
        scatter_piece(lax.dynamic_index_in_dim(x, chip, 0, keepdims=False), n_seq, k)
        for k, chip in chip_turns(n_seq)
    )


def spread_seq(x, n_seq):
    n_y = n_seq // 2
    me = lax.axis_index("seq")
    y, c = me // 2, me % 2
    x = x.reshape((n_y, 2) + x.shape[1:])
    out = jnp.zeros((n_seq,) + x.shape[2:], x.dtype)
    for k, chip in chip_turns(n_seq):
        pair = lax.dynamic_index_in_dim(x, chip, 0, keepdims=False)
        if k:
            pair = shift_chip(pair, n_seq, k)
        other = swap_core(lax.dynamic_index_in_dim(pair, 1 - c, 0, keepdims=False), n_seq)
        same = lax.dynamic_index_in_dim(pair, c, 0, keepdims=False)
        at = (y + n_y - k) % n_y * 2
        out = lax.dynamic_update_slice_in_dim(out, same[None], at + c, 0)
        out = lax.dynamic_update_slice_in_dim(out, other[None], at + 1 - c, 0)
    return out


def shift(x, axis, count, k):
    return lax.ppermute(x, axis, [(i, (i + k) % count) for i in range(count)])


def column_fold(x, op):
    rows, width = x.shape
    return op(x.reshape(rows // 8, 8, width), axis=0)


def attend_kernel(
    prompt_blocks, q_ref, k_ref, v_ref, segq_ref, segk_ref, o_ref, p_ref, inv_ref, krow, scores
):
    i = pl.program_id(1)
    group, qb = q_ref.shape[1], q_ref.shape[3]
    width = group * qb

    @pl.when(i == 0)
    def _():
        krow[...] = k_ref[0].astype(F32).T.astype(BF16)

    q = jnp.concatenate([q_ref[0, h] for h in range(group)], axis=1)
    segq = jnp.concatenate([segq_ref[...]] * group, axis=1)
    placeq = i * qb + lax.broadcasted_iota(jnp.int32, (1, width), 1) % qb

    def score(j, peak, masked):
        rows = pl.ds(pl.multiple_of(j * qb, qb), qb)
        s = dot(krow[rows, :], q)
        if masked:
            segk = segk_ref[rows, :]
            placek = j * qb + lax.broadcasted_iota(jnp.int32, (qb, 1), 0)
            keep = (placek <= placeq) & ((segk < 0) | (segk == segq))
            s = jnp.where(keep, s, NEG)
        scores[rows, :] = s
        return jnp.maximum(peak, column_fold(s, jnp.max))

    free = jnp.minimum(i, prompt_blocks)
    peak = jnp.full((8, width), NEG, F32)
    peak = lax.fori_loop(0, free, lambda j, m: score(j, m, False), peak)
    peak = lax.fori_loop(free, i + 1, lambda j, m: score(j, m, True), peak)
    peak = jnp.max(peak, axis=0, keepdims=True)

    def weigh(j, carry):
        total, acc = carry
        rows = pl.ds(pl.multiple_of(j * qb, qb), qb)
        p = jnp.exp(scores[rows, :] - peak)
        low = p.astype(BF16)
        p_ref[0, 0, rows, :] = low
        return total + column_fold(p, jnp.sum), acc + dot(v_ref[0, :, rows], low)

    total, acc = lax.fori_loop(
        0, i + 1, weigh, (jnp.zeros((8, width), F32), jnp.zeros((HEAD, width), F32))
    )
    inverse = 1.0 / jnp.sum(total, axis=0, keepdims=True)
    inv_ref[0, 0] = inverse
    out = (acc * inverse).astype(BF16)
    for h in range(group):
        o_ref[0, h] = out[:, h * qb : (h + 1) * qb]


def attend(qt, kt, vt, segment, prompt_len, block):
    kv, group, _, total = qt.shape
    blocks = total // block
    width = group * block
    pairs = kv * group * total * total // 2
    return pl.pallas_call(
        functools.partial(attend_kernel, prompt_len // block),
        grid=(kv, blocks),
        in_specs=[
            pl.BlockSpec((1, group, HEAD, block), lambda b, i: (b, 0, 0, i)),
            pl.BlockSpec((1, HEAD, total), lambda b, i: (b, 0, 0)),
            pl.BlockSpec((1, HEAD, total), lambda b, i: (b, 0, 0)),
            pl.BlockSpec((1, block), lambda b, i: (0, i)),
            pl.BlockSpec((total, 1), lambda b, i: (0, 0)),
        ],
        out_specs=[
            pl.BlockSpec((1, group, HEAD, block), lambda b, i: (b, 0, 0, i)),
            pl.BlockSpec((1, 1, total, width), lambda b, i: (b, i, 0, 0)),
            pl.BlockSpec((1, 1, 1, width), lambda b, i: (b, i, 0, 0)),
        ],
        out_shape=[
            jax.ShapeDtypeStruct(qt.shape, BF16),
            jax.ShapeDtypeStruct((kv, blocks, total, width), BF16),
            jax.ShapeDtypeStruct((kv, blocks, 1, width), F32),
        ],
        scratch_shapes=[pltpu.VMEM((total, HEAD), BF16), pltpu.VMEM((total, width), F32)],
        compiler_params=pltpu.CompilerParams(vmem_limit_bytes=40 * 2**20),
        cost_estimate=pl.CostEstimate(
            flops=pairs * HEAD * 4, bytes_accessed=pairs * 4, transcendentals=pairs
        ),
    )(qt, kt, vt, segment[None, :], segment[:, None])


def unrotate(grad, cosine, sine):
    half = HEAD // 2
    first, second = grad[:half], grad[half:]
    return jnp.concatenate(
        [first * cosine + second * sine, second * cosine - first * sine], axis=0
    )


def attend_back_kernel(
    q_ref, k_ref, v_ref, o_ref, do_ref, p_ref, inv_ref, cosq_ref, sinq_ref, cos_ref, sin_ref,
    dq_ref, dk_ref, dv_ref, vrow, dk_acc, dv_acc,
):
    i = pl.program_id(1)
    group, qb = q_ref.shape[1], q_ref.shape[3]
    width = group * qb

    @pl.when(i == 0)
    def _():
        vrow[...] = v_ref[0].astype(F32).T.astype(BF16)
        dk_acc[...] = jnp.zeros_like(dk_acc)
        dv_acc[...] = jnp.zeros_like(dv_acc)

    def side(ref, *at):
        return jnp.concatenate([ref[(0, *at, h)].astype(F32) for h in range(group)], axis=1)

    do = side(do_ref, 0) * inv_ref[0, 0]
    centre = jnp.sum(side(o_ref) * do, axis=0, keepdims=True)
    do_low = do.astype(BF16)
    do_rows = do.T.astype(BF16)
    q_rows = side(q_ref).T.astype(BF16)

    def step(j, acc):
        rows = pl.ds(pl.multiple_of(j * qb, qb), qb)
        p = p_ref[0, 0, rows, :]
        dp = dot(vrow[rows, :], do_low)
        ds = (p.astype(F32) * (dp - centre)).astype(BF16)
        dk_acc[rows, :] += dot(ds, q_rows)
        dv_acc[rows, :] += dot(p, do_rows)
        return acc + dot(k_ref[0, :, rows], ds)

    dq = lax.fori_loop(0, i + 1, step, jnp.zeros((HEAD, width), F32)) * HEAD**-0.5
    for h in range(group):
        part = dq[:, h * qb : (h + 1) * qb]
        dq_ref[0, h] = unrotate(part, cosq_ref[...], sinq_ref[...]).astype(BF16)

    @pl.when(i == pl.num_programs(1) - 1)
    def _():
        dk_ref[0] = unrotate(dk_acc[...].T, cos_ref[...], sin_ref[...]).astype(BF16)
        dv_ref[0] = dv_acc[...].T.astype(BF16)


def attend_back(qt, kt, vt, ot, do, p, inverse, cosine, sine):
    kv, group, _, total = qt.shape
    blocks, block = do.shape[0], do.shape[-1]
    width = group * block
    pairs = kv * group * total * total // 2
    q_spec = pl.BlockSpec((1, group, HEAD, block), lambda b, i: (b, 0, 0, i))
    k_spec = pl.BlockSpec((1, HEAD, total), lambda b, i: (b, 0, 0))
    return pl.pallas_call(
        attend_back_kernel,
        grid=(kv, blocks),
        in_specs=[
            q_spec, k_spec, k_spec, q_spec,
            pl.BlockSpec((1, 1, group, HEAD, block), lambda b, i: (i, b, 0, 0, 0)),
            pl.BlockSpec((1, 1, total, width), lambda b, i: (b, i, 0, 0)),
            pl.BlockSpec((1, 1, 1, width), lambda b, i: (b, i, 0, 0)),
            pl.BlockSpec((HEAD // 2, block), lambda b, i: (0, i)),
            pl.BlockSpec((HEAD // 2, block), lambda b, i: (0, i)),
            pl.BlockSpec((HEAD // 2, total), lambda b, i: (0, 0)),
            pl.BlockSpec((HEAD // 2, total), lambda b, i: (0, 0)),
        ],
        out_specs=[q_spec, k_spec, k_spec],
        out_shape=[
            jax.ShapeDtypeStruct(qt.shape, BF16),
            jax.ShapeDtypeStruct(kt.shape, BF16),
            jax.ShapeDtypeStruct(vt.shape, BF16),
        ],
        scratch_shapes=[
            pltpu.VMEM((total, HEAD), BF16),
            pltpu.VMEM((total, HEAD), F32),
            pltpu.VMEM((total, HEAD), F32),
        ],
        compiler_params=pltpu.CompilerParams(vmem_limit_bytes=40 * 2**20),
        cost_estimate=pl.CostEstimate(
            flops=pairs * HEAD * 8, bytes_accessed=pairs * 4, transcendentals=0
        ),
    )(qt, kt, vt, ot, do, p, inverse, cosine, sine, cosine, sine)


def pack_experts(gate_up, down):
    parts = [gate_up[..., :HIDDEN], gate_up[..., HIDDEN:]]
    parts += [down[..., m : m + HIDDEN] for m in range(0, MODEL_WIDTH, HIDDEN)]
    return jnp.concatenate(parts, axis=1)


def expert_kernel(
    starts, rows, hidden_rows, experts_all, first, last, place_ref, x_ref, dy_ref, gate_ref,
    zbias_ref, sbias_ref, dfa_ref, back_ref, *refs,
):
    refs = list(refs)
    carried = [None] * 5 if first else [refs.pop(0) for _ in range(5)]
    shards = [refs.pop(0) for _ in starts]
    outs = [refs.pop(0) for _ in range(5)]
    w_up, w_down, *accs, sem = refs
    count = w_up.shape[0]
    tile = x_ref.shape[0]

    def copies(e):
        pairs = []
        for b, (start, shard) in enumerate(zip(starts, shards)):
            index = place_ref[2 + b]
            up_rows = pl.ds(pl.multiple_of(index * rows, rows), rows)
            down_rows = pl.ds(pl.multiple_of(index * hidden_rows, hidden_rows), hidden_rows)
            for m in range(2):
                pairs.append((shard.at[start + e, pl.ds(m * rows, rows), :],
                              w_up.at[e, up_rows, pl.ds(m * HIDDEN, HIDDEN)]))
            for m in range(MODEL_WIDTH // HIDDEN):
                pairs.append((shard.at[start + e, pl.ds(2 * rows + m * hidden_rows, hidden_rows), :],
                              w_down.at[e, down_rows, pl.ds(m * HIDDEN, HIDDEN)]))
        return [pltpu.make_async_copy(a, b, sem.at[e, n]) for n, (a, b) in enumerate(pairs)]

    lane = lax.broadcasted_iota(jnp.int32, (tile, LANES), 1)

    def add(n, e, value):
        base = carried[n] if e == 0 else accs[n]
        if base is not None:
            value = base[...].astype(F32) + value
        if e < count - 1:
            accs[n][...] = value
        elif n == 2 and last:
            accs[n][...] = value
        elif n == 1 and last:
            outs[n][:, :MODEL_WIDTH] = value.astype(outs[n].dtype)
        else:
            outs[n][...] = value.astype(outs[n].dtype)

    def step(e):
        name = place_ref[0] + e
        both = dot(x_ref[...], w_up[e]) + zbias_ref[...]
        gate_in, up = both[:, :HIDDEN], both[:, HIDDEN:]
        sigma = jax.nn.sigmoid(gate_in)
        silu = gate_in * sigma
        inner = silu * up
        d_down = dot_nt(dy_ref[...], w_down[e]) + sbias_ref[...]
        d_gating = jnp.sum(inner * d_down, axis=1, keepdims=True)
        gating = jnp.sum(jnp.where(lane == name, gate_ref[...], 0.0), axis=1, keepdims=True)
        add(2, e, jnp.where((lane == name) | (lane == name + experts_all), d_gating, 0.0))
        gated = gating * inner
        add(3, e, gated)
        add(0, e, dot(gated.astype(BF16), w_down[e]))
        d_inner = gating * d_down
        d_gate = d_inner * up * (sigma + silu * (1.0 - sigma))
        d_both = jnp.concatenate([d_gate, d_inner * silu], axis=1)
        add(4, e, d_both)
        add(1, e, dot_nt(d_both.astype(BF16), w_up[e]))

    @pl.when(pl.program_id(0) == 0)
    def _():
        for e in range(count):
            for copy in copies(e):
                copy.start()
        for e in range(count):
            for copy in copies(e):
                copy.wait()
            step(e)

    @pl.when(pl.program_id(0) > 0)
    def _():
        for e in range(count):
            step(e)

    if last:
        aux = accs[2][...] + dot(outs[3][...], dfa_ref[...]) + dot(outs[4][...], back_ref[...])
        high = aux.astype(BF16)
        rest = (aux - high.astype(F32)).astype(BF16)
        is_rest = (lane >= experts_all) & (lane < 2 * experts_all)
        outs[1][:, MODEL_WIDTH:] = jnp.where(is_rest, rest, high)
        outs[2][...] = aux


def run_experts(place, x, dy, gates, zbias, sbias, mats, carried, shards, starts, count, experts_all, rows_out, last):
    rows = MODEL_WIDTH // len(shards)
    hidden_rows = HIDDEN // len(shards)
    first = carried is None
    acc_widths = (MODEL_WIDTH, MODEL_WIDTH, LANES, HIDDEN, 2 * HIDDEN)
    widths = (MODEL_WIDTH, MODEL_WIDTH + LANES if last else MODEL_WIDTH, *acc_widths[2:])
    dtypes = (BF16, BF16, F32, BF16, BF16)

    def tiled(width):
        return pl.BlockSpec((TILE, width), lambda t, place: (place[1] + t, 0))

    def out_tiled(width):
        return pl.BlockSpec((TILE, width), lambda t, _: (t, 0))

    in_widths = (MODEL_WIDTH, MODEL_WIDTH, LANES, 2 * HIDDEN, HIDDEN)
    specs = [tiled(w) for w in in_widths]
    specs += [pl.BlockSpec(m.shape, lambda t, _: (0, 0)) for m in mats]
    specs += [] if first else [tiled(w) for w in acc_widths]
    specs += [pl.BlockSpec(memory_space=pl.ANY)] * len(shards)
    copies = len(shards) * (2 + MODEL_WIDTH // HIDDEN)
    return pl.pallas_call(
        functools.partial(
            expert_kernel, tuple(starts), rows, hidden_rows, experts_all, first, last
        ),
        grid_spec=pltpu.PrefetchScalarGridSpec(
            num_scalar_prefetch=1,
            grid=(rows_out // TILE,),
            in_specs=specs,
            out_specs=[out_tiled(w) for w in widths],
            scratch_shapes=[
                pltpu.VMEM((count, MODEL_WIDTH, 2 * HIDDEN), BF16),
                pltpu.VMEM((count, HIDDEN, MODEL_WIDTH), BF16),
                *[pltpu.VMEM((TILE, w), F32) for w in acc_widths],
                pltpu.SemaphoreType.DMA((count, copies)),
            ],
        ),
        out_shape=[jax.ShapeDtypeStruct((rows_out, w), t) for w, t in zip(widths, dtypes)],
        compiler_params=pltpu.CompilerParams(vmem_limit_bytes=60 * 2**20),
        cost_estimate=pl.CostEstimate(
            flops=12 * rows_out * MODEL_WIDTH * HIDDEN * count,
            bytes_accessed=rows_out * MODEL_WIDTH * 10,
            transcendentals=rows_out * HIDDEN * count,
        ),
    )(place, x, dy, gates, zbias, sbias, *mats, *(carried or ()), *shards)


def norm_backward(value_rows, inverse, gain_row, upstream):
    scaled = upstream * gain_row
    inner_mean = jnp.mean(value_rows * scaled, axis=-1, keepdims=True)
    return inverse * scaled - value_rows * (inverse * inverse * inverse) * inner_mean


def layout(lengths_row, prompt_len, total_len):
    ends = jnp.sum(jnp.tril(jnp.ones((lengths_row.shape[0],) * 2, jnp.int32)) * lengths_row, axis=1)
    starts = ends - lengths_row
    places = jnp.arange(total_len, dtype=jnp.int32)
    offset = places - prompt_len
    counted = jnp.sum((offset[:, None] >= ends[None, :]).astype(jnp.int32), axis=1)
    inside = offset >= 0
    segment = jnp.where(inside, counted, -1)
    picked = jnp.arange(lengths_row.shape[0], dtype=jnp.int32)[None, :] == counted[:, None]
    begin = jnp.sum(jnp.where(picked, starts[None, :], 0), axis=1)
    position = jnp.where(inside, prompt_len + offset - begin, places)
    return (segment, position)


def pad_lanes(x, at=0, width=LANES):
    return jnp.pad(x, ((0, 0), (at, width - at - x.shape[1])))


def gather_groups(x, n_dp, n_wt):
    row = jnp.stack([shift(x, "dp", n_dp, k) if k else x for k in range(n_dp)])
    return jnp.concatenate([shift(row, "wt", n_wt, b) if b else row for b in range(n_wt)])


def reduce_seq(flat, n_seq):
    rows, width = flat.shape
    return scatter_seq(flat.reshape(n_seq, rows // n_seq, width), n_seq)


def tagged(mine, index_now):
    return jnp.concatenate([mine, jnp.full((8, mine.shape[1]), index_now.astype(F32))], 0)


def by_adapter(everyone, names, n_seq, n_wt):
    share = ADAPTER_COUNT // n_wt
    part, width = everyone.shape[1:]
    first_row = lax.axis_index("wt") * share
    picks = (names[None, :] == first_row + jnp.arange(share)[:, None]).astype(F32)
    kept = jnp.sum(picks[:, :, None, None] * everyone[None].astype(F32), axis=1)
    pieces = seq_pieces(kept.reshape(share * part, width), n_seq)
    place = jnp.arange(n_seq)[None, :, None, None]
    full = sum(jnp.where(place == at, x.reshape(share, 1, part, width), 0.0) for at, x in pieces)
    return full.reshape(share, n_seq * part, width)


def shards(
    tokens,
    cotangent,
    routes,
    lengths,
    group_adapter_index,
    attention_norm_gain,
    query_weight,
    key_value_weight,
    output_weight,
    mixture_norm_gain,
    router_weight,
    expert_gate_up_weight,
    expert_down_weight,
    attention_first_factors,
    query_second_factor,
    key_value_second_factors,
    output_first_factor,
    output_second_factor,
    mixture_first_factors,
    router_second_factor,
    gate_up_second_factors,
    down_first_factor,
    down_second_factor,
):
    n_seq, n_dp, n_wt = (lax.axis_size(a) for a in ("seq", "dp", "wt"))
    seq, dp, wt = (lax.axis_index(a) for a in ("seq", "dp", "wt"))
    local = tokens.shape[1]
    total = local * n_seq
    prompt_len = max(PROMPT_LEAST, PROMPT_DEV * n_seq)
    exp_dev = expert_gate_up_weight.shape[0]
    experts_all = exp_dev * n_seq
    kv_local = KV_HEADS // n_seq
    group = HEADS // KV_HEADS
    q_width = MODEL_WIDTH // n_seq
    k_width = KEY_FEATURES // n_seq
    rank = ADAPTER_RANK
    index_now = group_adapter_index[0]

    def chosen(bank):
        return lax.dynamic_index_in_dim(bank, index_now, 0, keepdims=False)

    def own(x, size, axis=1, at=0):
        return lax.dynamic_slice_in_dim(x, at + seq * size, size, axis)

    attn_first = chosen(attention_first_factors)
    query_second = own(chosen(query_second_factor), q_width)
    kv_second = chosen(key_value_second_factors)
    out_first = chosen(output_first_factor)
    out_second = chosen(output_second_factor)
    mix_first = chosen(mixture_first_factors)
    router_second = chosen(router_second_factor)
    gate_up_second = chosen(gate_up_second_factors)
    down_first = chosen(down_first_factor)
    down_second = chosen(down_second_factor)

    def own_rows(x):
        return lax.dynamic_slice_in_dim(x, seq * local, local, 0)

    split = FIRST_EXPERTS
    tie = lax.optimization_barrier

    def across(x):
        return [shift(x, "dp", n_dp, k) for k in range(1, n_dp)]

    came = pack_experts(expert_gate_up_weight, expert_down_weight)
    pieces = [(0, 0, came)]
    for b in range(1, n_wt - 1):
        came, *moved = tie((shift(came, "wt", n_wt, 1), *across(came)))
        pieces += [(k, b - 1, x) for k, x in enumerate(moved, 1)] + [(0, b, came)]
    ahead, *moved = tie((shift(came[:split], "wt", n_wt, 1), *across(came)))
    pieces += [(k, n_wt - 2, x) for k, x in enumerate(moved, 1)]
    behind = shift(came[split:], "wt", n_wt, 1)
    ahead = [ahead, *across(ahead)]
    behind = [behind, *across(behind)]

    hidden = gather_seq(tokens[0], n_seq).reshape(total, MODEL_WIDTH)

    def gather_weights(x):
        return lax.all_gather(x, ("dp", "wt"), axis=0, tiled=True)

    mine = jnp.concatenate(
        [
            own(query_weight, q_width),
            own(key_value_weight, k_width),
            own(key_value_weight, k_width, at=KEY_FEATURES),
            pad_lanes(router_weight),
        ],
        axis=1,
    )
    gathered = gather_weights(mine)
    qkv_width = q_width + 2 * k_width
    qkv_weight = gathered[:, :qkv_width]
    router_full = gathered[:, qkv_width : qkv_width + experts_all]
    half = MODEL_WIDTH // 2
    core = seq % 2
    out_mine = gather_weights(lax.dynamic_slice_in_dim(output_weight, core * half, half, 1))
    out_other = swap_core(out_mine, n_seq)
    out_weight = jnp.where(
        core == 0,
        jnp.concatenate([out_mine, out_other], 1),
        jnp.concatenate([out_other, out_mine], 1),
    )

    gain_first = attention_norm_gain.astype(F32)
    gain_second = mixture_norm_gain.astype(F32)
    hidden_f = hidden.astype(F32)
    inverse_a = lax.rsqrt(jnp.mean(hidden_f * hidden_f, axis=-1, keepdims=True) + EPS)
    normed = (hidden_f * inverse_a * gain_first).astype(BF16)
    small_a = dot(normed, attn_first).astype(BF16)
    second = jnp.zeros((3 * rank, qkv_width), BF16)
    second = second.at[:rank, :q_width].set(query_second)
    second = second.at[rank : 2 * rank, q_width : q_width + k_width].set(own(kv_second[0], k_width))
    second = second.at[2 * rank :, q_width + k_width :].set(own(kv_second[1], k_width))
    qkv = dot(qkv_weight, normed, ((0,), (1,))) + dot(second, small_a, ((0,), (1,)))
    segment, position = layout(lengths[0], prompt_len, total)
    freq = jnp.exp(jnp.arange(HEAD // 2, dtype=F32) * (-2.0 * math.log(10000.0) / HEAD))
    angle = freq[:, None] * position.astype(F32)[None, :]
    cosine, sine = jnp.cos(angle), jnp.sin(angle)

    def rotate(x, scale=1.0):
        x = x.reshape(-1, 2, HEAD // 2, total)
        a, b = x[:, 0], x[:, 1]
        x = jnp.concatenate([a * cosine - b * sine, b * cosine + a * sine], axis=1)
        return (x.astype(BF16) * jnp.asarray(scale, BF16)).reshape(-1, HEAD, total)

    qt = rotate(qkv[:q_width], HEAD**-0.5).reshape(kv_local, group, HEAD, total)
    kt = rotate(qkv[q_width : q_width + k_width])
    vt = qkv[q_width + k_width :].astype(BF16).reshape(kv_local, HEAD, total)
    ot, probs, inverse_l = attend(qt, kt, vt, segment, prompt_len, local)
    att = gather_seq(ot.reshape(q_width, total), n_seq).reshape(MODEL_WIDTH, total)

    named = jnp.arange(LANES, dtype=jnp.int32)[None, None, :]
    mask = jnp.any(routes[0][:, :, None] == named, axis=1).astype(BF16)
    d_out = jnp.concatenate([cotangent[0], mask], axis=1)
    d_out, _ = lax.optimization_barrier((d_out, hidden))
    d_out = gather_seq(d_out, n_seq).reshape(total, MODEL_WIDTH + LANES)
    d_out_all = d_out[:, :MODEL_WIDTH]
    routed = d_out[:, MODEL_WIDTH : MODEL_WIDTH + experts_all] > 0.5

    small_o = dot_tn(att, out_first).astype(BF16)
    residual = hidden_f + dot_tn(att, out_weight) + dot(small_o, out_second)
    inverse_m = lax.rsqrt(jnp.mean(residual * residual, axis=-1, keepdims=True) + EPS)
    normed_m = (residual * inverse_m * gain_second).astype(BF16)
    mix_router = jnp.concatenate([mix_first, router_full], axis=1)
    states = dot(normed_m, mix_router)
    small_m = states[:, : 3 * rank].astype(BF16)
    logits = states[:, 3 * rank :] + dot(small_m[:, :rank], router_second)
    logits = jnp.where(routed, logits, NEG)
    peak = jnp.max(logits, axis=-1, keepdims=True)
    weights = jnp.where(routed, jnp.exp(logits - peak), 0.0)
    gating = weights / jnp.sum(weights, axis=-1, keepdims=True)

    d_rank = dot_nt(d_out_all, down_second).astype(BF16)
    gus = jnp.zeros((2 * rank, 2 * HIDDEN), BF16)
    gus = gus.at[:rank, :HIDDEN].set(gate_up_second[0])
    gus = gus.at[rank:, HIDDEN:].set(gate_up_second[1])
    mats = (pad_lanes(down_first, DOWN_AT), pad_lanes(gus.T, SMALL_AT))
    zbias = dot(small_m[:, rank:], gus).astype(BF16)
    sbias = dot_nt(d_rank, down_first).astype(BF16)
    gates = pad_lanes(gating)

    order = [(k, b) for k, b, _ in pieces] + [(k, n_wt - 1) for k in range(n_dp)]
    places = [(dp + n_dp - k) % n_dp * n_wt + (wt + n_wt - b) % n_wt for k, b in order]
    held = [x for _, _, x in pieces]

    def place_of(expert, row):
        return jnp.stack([x.astype(jnp.int32) for x in (seq * exp_dev + expert, row, *places)])

    carried = run_experts(
        place_of(0, seq * 0), normed_m, d_out_all, gates, zbias, sbias, mats, None, held + ahead,
        [0] * len(order), split, experts_all, total, False,
    )
    chip_rows = 2 * local
    turns, arrived, waiting = [], [], None
    for k, chip in chip_turns(n_seq):
        place = place_of(split, chip * (chip_rows // TILE))
        if waiting is not None:
            place, sent = tie((place, waiting[1].astype(BF16)))
            arrived.append(shift_chip(sent, n_seq, waiting[0]))
        parts = run_experts(
            place, normed_m, d_out_all, gates, zbias, sbias, mats, carried, held + behind,
            [split] * len(held) + [0] * len(behind), exp_dev - split, experts_all, chip_rows, True,
        )
        parts = list(parts)
        if arrived:
            arrived[-1], parts[1] = tie((arrived[-1], parts[1]))
        turns.append((k, chip, parts))
        waiting = (k, core_sum(parts[1].reshape(2, local, -1), n_seq))
    back_sum = waiting[1] + sum(x.astype(F32) for x in arrived)

    upstream = cotangent[0].astype(F32)
    residual_own = own_rows(residual)
    gating_own = own_rows(gating)
    small_m_own = own_rows(small_m)
    d_gating = (
        back_sum[:, MODEL_WIDTH : MODEL_WIDTH + experts_all]
        + back_sum[:, MODEL_WIDTH + experts_all : MODEL_WIDTH + 2 * experts_all]
    )
    d_logits = gating_own * (d_gating - jnp.sum(d_gating * gating_own, axis=-1, keepdims=True))
    d_logits_low = d_logits.astype(BF16)
    d_small_m = jnp.concatenate(
        [dot_nt(d_logits_low, router_second), back_sum[:, MODEL_WIDTH + SMALL_AT :]], axis=1
    ).astype(BF16)
    small_d = back_sum[:, MODEL_WIDTH + DOWN_AT : MODEL_WIDTH + DOWN_AT + rank].astype(BF16)
    d_normed_m = back_sum[:, :MODEL_WIDTH] + dot_nt(
        jnp.concatenate([d_small_m, d_logits_low], axis=1), mix_router
    )
    d_residual = upstream + norm_backward(
        residual_own, own_rows(inverse_m), gain_second, d_normed_m
    )
    d_branch = d_residual.astype(BF16)
    d_small_o = dot_nt(d_branch, out_second).astype(BF16)
    d_att = (dot_nt(out_weight, d_branch) + dot_nt(out_first, d_small_o)).astype(BF16)
    d_att = spread_seq(d_att.reshape(n_seq, q_width, local), n_seq)

    def of_chip(x, chip, axis=0):
        return lax.dynamic_slice_in_dim(x, chip * chip_rows, chip_rows, axis)

    grad_gu = sum(dot_tn(of_chip(small_m[:, rank:], chip), parts[4]) for _, chip, parts in turns)
    grad_down = sum(dot_tn(of_chip(d_rank, chip), parts[3]) for _, chip, parts in turns)
    att_own = lax.dynamic_slice_in_dim(att, seq * local, local, 1)
    early = jnp.concatenate(
        [
            dot(d_small_o, att_own, ((0,), (1,))),
            dot_tn(own_rows(small_o), d_branch),
            dot_tn(d_small_m, own_rows(normed_m)),
            dot_tn(small_d, cotangent[0]),
            jnp.concatenate([grad_gu[:rank, :HIDDEN], grad_gu[rank:, HIDDEN:], grad_down], axis=1),
            pad_lanes(dot_tn(small_m_own[:, :rank], d_logits_low), width=MODEL_WIDTH),
        ],
        axis=0,
    )
    early = reduce_seq(early, n_seq)
    parts_out = [core_sum(parts[0].reshape(2, local, -1), n_seq) for _, _, parts in turns]
    early, d_att, *parts_sent = tie((early, d_att, *[x.astype(BF16) for x in parts_out[:-1]]))
    early = lax.all_gather(tagged(early, index_now), ("dp", "wt"), axis=0)
    sent = [shift_chip(x, n_seq, k) for x, (k, _, _) in zip(parts_sent, turns)]
    dqt, dkt, dvt = attend_back(
        qt, kt, vt, ot, d_att.reshape(n_seq, kv_local, group, HEAD, local), probs, inverse_l,
        cosine, sine,
    )
    dqt, *sent = tie((dqt, *sent))
    output_rows = residual_own + dot(small_d, down_second) + parts_out[-1]
    output_rows = output_rows + sum(x.astype(F32) for x in sent)

    d_qkv = jnp.concatenate(
        [dqt.reshape(q_width, total), dkt.reshape(k_width, total), dvt.reshape(k_width, total)], 0
    )
    d_small_a = dot(d_qkv, second, ((0,), (1,))).astype(BF16)
    grad_second = dot(small_a, d_qkv, ((0,), (1,)))

    def spread(x, width, full):
        return lax.dynamic_update_slice_in_dim(
            jnp.zeros((x.shape[0], full), F32), x, seq * width, 1
        )

    late = jnp.concatenate(
        [
            dot_tn(d_small_a, normed),
            spread(grad_second[:rank, :q_width], q_width, MODEL_WIDTH),
            jnp.concatenate(
                [
                    spread(grad_second[rank : 2 * rank, q_width : q_width + k_width], k_width, KEY_FEATURES),
                    spread(grad_second[2 * rank :, q_width + k_width :], k_width, KEY_FEATURES),
                    jnp.zeros((rank, MODEL_WIDTH - 2 * KEY_FEATURES), F32),
                ],
                axis=1,
            ),
        ],
        axis=0,
    )
    late = reduce_seq(late, n_seq)
    d_normed = None
    for k, chip in chip_turns(n_seq):
        part = dot(of_chip(d_qkv, chip, 1), qkv_weight, ((0,), (1,)))
        part = part + dot_nt(of_chip(d_small_a, chip), attn_first)
        part = core_sum(part.astype(BF16).reshape(2, local, MODEL_WIDTH), n_seq)
        if k:
            late, part = tie((late, part.astype(BF16)))
            part = shift_chip(part, n_seq, k).astype(F32)
        d_normed = part if d_normed is None else d_normed + part
    input_grad = d_residual + norm_backward(
        tokens[0].astype(F32), own_rows(inverse_a), gain_first, d_normed
    )
    names = early[:, -1, 0].astype(jnp.int32)
    early = by_adapter(early[:, :-8], names, n_seq, n_wt)
    turned = jnp.stack(
        [
            (dp + n_dp - k) % n_dp * n_wt + (wt + n_wt - b) % n_wt
            for b in range(n_wt) for k in range(n_dp)
        ]
    )
    late = by_adapter(gather_groups(late.astype(BF16), n_dp, n_wt), names[turned], n_seq, n_wt)

    def flip(x):
        return jnp.swapaxes(x, 1, 2)

    def at(flat, row, count, lo=0, hi=MODEL_WIDTH):
        return flat[:, row : row + count, lo:hi]

    low = 6 * rank
    return (
        output_rows[None].astype(BF16),
        input_grad[None],
        flip(at(late, 0, 3 * rank)),
        at(late, 3 * rank, rank),
        jnp.stack(
            [at(late, 4 * rank, rank, m, m + KEY_FEATURES) for m in (0, KEY_FEATURES)], axis=1
        ),
        flip(at(early, 0, rank)),
        at(early, rank, rank),
        flip(at(early, 2 * rank, 3 * rank)),
        at(early, low + rank, rank, 0, experts_all),
        jnp.stack([at(early, low, rank, m, m + HIDDEN) for m in (0, HIDDEN)], axis=1),
        flip(at(early, low, rank, 2 * HIDDEN, 3 * HIDDEN)),
        at(early, 5 * rank, rank),
    )


def solution(mesh):
    split = P(("dp", "wt"), "seq", None)
    rows = P(("dp", "wt"), None)
    bank = P("wt", None, None)
    placed = (
        split, split, split, rows, P(("dp", "wt")), P(), rows, rows, rows, P(), rows,
        P("seq", ("dp", "wt"), None), P("seq", ("dp", "wt"), None),
    ) + (P(),) * 10
    wide = P("wt", None, None, None)
    return jax.shard_map(
        shards,
        mesh=mesh,
        in_specs=placed,
        out_specs=(split, split, bank, bank, wide, bank, bank, bank, bank, wide, bank, bank),
        check_vma=False,
    )
```

```python
import functools
import math

import jax
import jax.numpy as jnp
from jax import lax
from jax.experimental import pallas as pl
from jax.experimental.pallas import tpu as pltpu
from jax.sharding import PartitionSpec as P

MODEL_WIDTH = 1536
HEADS = 24
KV_HEADS = 8
HEAD = 64
HIDDEN = 512
ADAPTER_RANK = 16
ADAPTER_COUNT = 8
PROMPT_LEAST = 1024
PROMPT_DEV = 128
KEY_FEATURES = 512
LANES = 128
SMALL_AT = 96

EPS = 1e-05
NEG = -1e30
F32 = jnp.float32
BF16 = jnp.bfloat16
FIRST_EXPERTS = 3
HOLD = 1
TILE = 256
DOWN_AT = 80


def dot(a, b, dims=((1,), (0,))):
    return lax.dot_general(a, b, (dims, ((), ())), preferred_element_type=F32)


def dot_nt(a, b):
    return dot(a, b, ((1,), (1,)))


def dot_tn(a, b):
    return dot(a, b, ((0,), (0,)))


def swap_core(x, n_seq):
    return lax.ppermute(x, "seq", [(i, i ^ 1) for i in range(n_seq)])


def shift_chip(x, n_seq, k):
    n_y = n_seq // 2
    pairs = [(y * 2 + c, (y + k) % n_y * 2 + c) for y in range(n_y) for c in range(2)]
    return lax.ppermute(x, "seq", pairs)


def seq_pieces(x, n_seq):
    n_y = n_seq // 2
    me = lax.axis_index("seq")
    y, c = me // 2, me % 2
    far = [shift_chip(x, n_seq, k) for k in range(1, n_y)]
    pieces = [(me, x), (me ^ 1, swap_core(x, n_seq))]
    for k, piece in enumerate(far, 1):
        chip = (y + n_y - k) % n_y * 2
        pieces += [(chip + c, piece), (chip + 1 - c, swap_core(piece, n_seq))]
    return pieces


def gather_seq(x, n_seq):
    out = jnp.zeros((n_seq,) + x.shape, x.dtype)
    for at, piece in seq_pieces(x, n_seq):
        out = lax.dynamic_update_slice_in_dim(out, piece[None], at, 0)
    return out


def core_sum(x, n_seq):
    c = lax.axis_index("seq") % 2
    got = swap_core(lax.dynamic_index_in_dim(x, 1 - c, 0, keepdims=False), n_seq)
    kept = lax.dynamic_index_in_dim(x, c, 0, keepdims=False)
    return kept.astype(F32) + got.astype(F32)


def scatter_piece(x, n_seq, k):
    both = core_sum(x, n_seq)
    return shift_chip(both.astype(x.dtype), n_seq, k).astype(F32) if k else both


def chip_turns(n_seq):
    n_y = n_seq // 2
    y = lax.axis_index("seq") // 2
    return [(k, (y + k) % n_y) for k in [*range(1, n_y), 0]]


def scatter_seq(x, n_seq):
    x = x.reshape((n_seq // 2, 2) + x.shape[1:])
    return sum(
        scatter_piece(lax.dynamic_index_in_dim(x, chip, 0, keepdims=False), n_seq, k)
        for k, chip in chip_turns(n_seq)
    )


def spread_seq(x, n_seq):
    n_y = n_seq // 2
    me = lax.axis_index("seq")
    y, c = me // 2, me % 2
    x = x.reshape((n_y, 2) + x.shape[1:])
    out = jnp.zeros((n_seq,) + x.shape[2:], x.dtype)
    for k, chip in chip_turns(n_seq):
        pair = lax.dynamic_index_in_dim(x, chip, 0, keepdims=False)
        if k:
            pair = shift_chip(pair, n_seq, k)
        other = swap_core(lax.dynamic_index_in_dim(pair, 1 - c, 0, keepdims=False), n_seq)
        same = lax.dynamic_index_in_dim(pair, c, 0, keepdims=False)
        at = (y + n_y - k) % n_y * 2
        out = lax.dynamic_update_slice_in_dim(out, same[None], at + c, 0)
        out = lax.dynamic_update_slice_in_dim(out, other[None], at + 1 - c, 0)
    return out


def shift(x, axis, count, k):
    return lax.ppermute(x, axis, [(i, (i + k) % count) for i in range(count)])


def column_fold(x, op):
    rows, width = x.shape
    return op(x.reshape(rows // 8, 8, width), axis=0)


def attend_kernel(
    prompt_blocks, q_ref, k_ref, v_ref, segq_ref, segk_ref, o_ref, p_ref, inv_ref, krow, scores
):
    i = pl.program_id(1)
    group, qb = q_ref.shape[1], q_ref.shape[3]
    width = group * qb

    @pl.when(i == 0)
    def _():
        krow[...] = k_ref[0].astype(F32).T.astype(BF16)

    q = jnp.concatenate([q_ref[0, h] for h in range(group)], axis=1)
    segq = jnp.concatenate([segq_ref[...]] * group, axis=1)
    placeq = i * qb + lax.broadcasted_iota(jnp.int32, (1, width), 1) % qb

    def score(j, peak, masked):
        rows = pl.ds(pl.multiple_of(j * qb, qb), qb)
        s = dot(krow[rows, :], q)
        if masked:
            segk = segk_ref[rows, :]
            placek = j * qb + lax.broadcasted_iota(jnp.int32, (qb, 1), 0)
            keep = (placek <= placeq) & ((segk < 0) | (segk == segq))
            s = jnp.where(keep, s, NEG)
        scores[rows, :] = s
        return jnp.maximum(peak, column_fold(s, jnp.max))

    free = jnp.minimum(i, prompt_blocks)
    peak = jnp.full((8, width), NEG, F32)
    peak = lax.fori_loop(0, free, lambda j, m: score(j, m, False), peak)
    peak = lax.fori_loop(free, i + 1, lambda j, m: score(j, m, True), peak)
    peak = jnp.max(peak, axis=0, keepdims=True)

    def weigh(j, carry):
        total, acc = carry
        rows = pl.ds(pl.multiple_of(j * qb, qb), qb)
        p = jnp.exp(scores[rows, :] - peak)
        low = p.astype(BF16)
        p_ref[0, 0, rows, :] = low
        return total + column_fold(p, jnp.sum), acc + dot(v_ref[0, :, rows], low)

    total, acc = lax.fori_loop(
        0, i + 1, weigh, (jnp.zeros((8, width), F32), jnp.zeros((HEAD, width), F32))
    )
    inverse = 1.0 / jnp.sum(total, axis=0, keepdims=True)
    inv_ref[0, 0] = inverse
    out = (acc * inverse).astype(BF16)
    for h in range(group):
        o_ref[0, h] = out[:, h * qb : (h + 1) * qb]


def attend(qt, kt, vt, segment, prompt_len, block):
    kv, group, _, total = qt.shape
    blocks = total // block
    width = group * block
    pairs = kv * group * total * total // 2
    return pl.pallas_call(
        functools.partial(attend_kernel, prompt_len // block),
        grid=(kv, blocks),
        in_specs=[
            pl.BlockSpec((1, group, HEAD, block), lambda b, i: (b, 0, 0, i)),
            pl.BlockSpec((1, HEAD, total), lambda b, i: (b, 0, 0)),
            pl.BlockSpec((1, HEAD, total), lambda b, i: (b, 0, 0)),
            pl.BlockSpec((1, block), lambda b, i: (0, i)),
            pl.BlockSpec((total, 1), lambda b, i: (0, 0)),
        ],
        out_specs=[
            pl.BlockSpec((1, group, HEAD, block), lambda b, i: (b, 0, 0, i)),
            pl.BlockSpec((1, 1, total, width), lambda b, i: (b, i, 0, 0)),
            pl.BlockSpec((1, 1, 1, width), lambda b, i: (b, i, 0, 0)),
        ],
        out_shape=[
            jax.ShapeDtypeStruct(qt.shape, BF16),
            jax.ShapeDtypeStruct((kv, blocks, total, width), BF16),
            jax.ShapeDtypeStruct((kv, blocks, 1, width), F32),
        ],
        scratch_shapes=[pltpu.VMEM((total, HEAD), BF16), pltpu.VMEM((total, width), F32)],
        compiler_params=pltpu.CompilerParams(vmem_limit_bytes=40 * 2**20),
        cost_estimate=pl.CostEstimate(
            flops=pairs * HEAD * 4, bytes_accessed=pairs * 4, transcendentals=pairs
        ),
    )(qt, kt, vt, segment[None, :], segment[:, None])


def unrotate(grad, cosine, sine):
    half = HEAD // 2
    first, second = grad[:half], grad[half:]
    return jnp.concatenate(
        [first * cosine + second * sine, second * cosine - first * sine], axis=0
    )


def attend_back_kernel(
    q_ref, k_ref, v_ref, o_ref, do_ref, p_ref, inv_ref, cosq_ref, sinq_ref, cos_ref, sin_ref,
    dq_ref, dk_ref, dv_ref, vrow, dk_acc, dv_acc,
):
    i = pl.program_id(1)
    group, qb = q_ref.shape[1], q_ref.shape[3]
    width = group * qb

    @pl.when(i == 0)
    def _():
        vrow[...] = v_ref[0].astype(F32).T.astype(BF16)
        dk_acc[...] = jnp.zeros_like(dk_acc)
        dv_acc[...] = jnp.zeros_like(dv_acc)

    def side(ref, *at):
        return jnp.concatenate([ref[(0, *at, h)].astype(F32) for h in range(group)], axis=1)

    do = side(do_ref, 0) * inv_ref[0, 0]
    centre = jnp.sum(side(o_ref) * do, axis=0, keepdims=True)
    do_low = do.astype(BF16)
    do_rows = do.T.astype(BF16)
    q_rows = side(q_ref).T.astype(BF16)

    def step(j, acc):
        rows = pl.ds(pl.multiple_of(j * qb, qb), qb)
        p = p_ref[0, 0, rows, :]
        dp = dot(vrow[rows, :], do_low)
        ds = (p.astype(F32) * (dp - centre)).astype(BF16)
        dk_acc[rows, :] += dot(ds, q_rows)
        dv_acc[rows, :] += dot(p, do_rows)
        return acc + dot(k_ref[0, :, rows], ds)

    dq = lax.fori_loop(0, i + 1, step, jnp.zeros((HEAD, width), F32)) * HEAD**-0.5
    for h in range(group):
        part = dq[:, h * qb : (h + 1) * qb]
        dq_ref[0, h] = unrotate(part, cosq_ref[...], sinq_ref[...]).astype(BF16)

    @pl.when(i == pl.num_programs(1) - 1)
    def _():
        dk_ref[0] = unrotate(dk_acc[...].T, cos_ref[...], sin_ref[...]).astype(BF16)
        dv_ref[0] = dv_acc[...].T.astype(BF16)


def attend_back(qt, kt, vt, ot, do, p, inverse, cosine, sine):
    kv, group, _, total = qt.shape
    blocks, block = do.shape[0], do.shape[-1]
    width = group * block
    pairs = kv * group * total * total // 2
    q_spec = pl.BlockSpec((1, group, HEAD, block), lambda b, i: (b, 0, 0, i))
    k_spec = pl.BlockSpec((1, HEAD, total), lambda b, i: (b, 0, 0))
    return pl.pallas_call(
        attend_back_kernel,
        grid=(kv, blocks),
        in_specs=[
            q_spec, k_spec, k_spec, q_spec,
            pl.BlockSpec((1, 1, group, HEAD, block), lambda b, i: (i, b, 0, 0, 0)),
            pl.BlockSpec((1, 1, total, width), lambda b, i: (b, i, 0, 0)),
            pl.BlockSpec((1, 1, 1, width), lambda b, i: (b, i, 0, 0)),
            pl.BlockSpec((HEAD // 2, block), lambda b, i: (0, i)),
            pl.BlockSpec((HEAD // 2, block), lambda b, i: (0, i)),
            pl.BlockSpec((HEAD // 2, total), lambda b, i: (0, 0)),
            pl.BlockSpec((HEAD // 2, total), lambda b, i: (0, 0)),
        ],
        out_specs=[q_spec, k_spec, k_spec],
        out_shape=[
            jax.ShapeDtypeStruct(qt.shape, BF16),
            jax.ShapeDtypeStruct(kt.shape, BF16),
            jax.ShapeDtypeStruct(vt.shape, BF16),
        ],
        scratch_shapes=[
            pltpu.VMEM((total, HEAD), BF16),
            pltpu.VMEM((total, HEAD), F32),
            pltpu.VMEM((total, HEAD), F32),
        ],
        compiler_params=pltpu.CompilerParams(vmem_limit_bytes=40 * 2**20),
        cost_estimate=pl.CostEstimate(
            flops=pairs * HEAD * 8, bytes_accessed=pairs * 4, transcendentals=0
        ),
    )(qt, kt, vt, ot, do, p, inverse, cosine, sine, cosine, sine)


def pack_experts(gate_up, down):
    count, _, _ = gate_up.shape
    rows = down.shape[1]
    parts = [gate_up[..., :HIDDEN], gate_up[..., HIDDEN:]]
    parts += [down[..., m : m + HIDDEN] for m in range(0, MODEL_WIDTH, HIDDEN)]
    return jnp.concatenate(parts, axis=1).reshape(count, 3, 3, rows, HIDDEN)


def expert_kernel(
    shards_count, experts_all, first, last, place_ref, x_ref, dy_ref, gate_ref,
    zbias_ref, sbias_ref, dfa_ref, back_ref, *refs,
):
    refs = list(refs)
    carried = [None] * 5 if first else [refs.pop(0) for _ in range(5)]
    shards = [refs.pop(0) for _ in range(shards_count)]
    outs = [refs.pop(0) for _ in range(5)]
    w_up, w_down, *accs, sem = refs
    count = w_up.shape[0]
    tile = x_ref.shape[0]

    def copies(e):
        pairs = []
        for b, shard in enumerate(shards):
            pairs.append((shard.at[e, pl.ds(0, 2)], w_up.at[e, :, place_ref[2 + b]]))
            pairs.append((shard.at[e, 2], w_down.at[e, :, place_ref[2 + b]]))
        return [pltpu.make_async_copy(a, b, sem.at[e, n]) for n, (a, b) in enumerate(pairs)]

    lane = lax.broadcasted_iota(jnp.int32, (tile, LANES), 1)

    def add(n, e, value):
        base = carried[n] if e == 0 else accs[n]
        if base is not None:
            value = base[...].astype(F32) + value
        if e < count - 1:
            accs[n][...] = value
        elif n == 2 and last:
            accs[n][...] = value
        elif n == 1 and last:
            outs[n][:, :MODEL_WIDTH] = value.astype(outs[n].dtype)
        else:
            outs[n][...] = value.astype(outs[n].dtype)

    def step(e):
        name = place_ref[0] + e
        up_weight = jnp.concatenate(
            [w_up[e, m].reshape(MODEL_WIDTH, HIDDEN) for m in range(2)], axis=1
        )
        down_weight = jnp.concatenate(
            [w_down[e, m].reshape(HIDDEN, HIDDEN) for m in range(MODEL_WIDTH // HIDDEN)], axis=1
        )
        both = dot(x_ref[...], up_weight) + zbias_ref[...]
        gate_in, up = both[:, :HIDDEN], both[:, HIDDEN:]
        sigma = jax.nn.sigmoid(gate_in)
        silu = gate_in * sigma
        inner = silu * up
        d_down = dot_nt(dy_ref[...], down_weight) + sbias_ref[...]
        d_gating = jnp.sum(inner * d_down, axis=1, keepdims=True)
        gating = jnp.sum(jnp.where(lane == name, gate_ref[...], 0.0), axis=1, keepdims=True)
        add(2, e, jnp.where((lane == name) | (lane == name + experts_all), d_gating, 0.0))
        gated = gating * inner
        add(3, e, gated)
        add(0, e, dot(gated.astype(BF16), down_weight))
        d_inner = gating * d_down
        d_gate = d_inner * up * (sigma + silu * (1.0 - sigma))
        d_both = jnp.concatenate([d_gate, d_inner * silu], axis=1)
        add(4, e, d_both)
        add(1, e, dot_nt(d_both.astype(BF16), up_weight))

    @pl.when(pl.program_id(0) == 0)
    def _():
        for e in range(count):
            for copy in copies(e):
                copy.start()
        for e in range(count):
            for copy in copies(e):
                copy.wait()
            step(e)

    @pl.when(pl.program_id(0) > 0)
    def _():
        for e in range(count):
            step(e)

    if last:
        aux = accs[2][...] + dot(outs[3][...], dfa_ref[...]) + dot(outs[4][...], back_ref[...])
        high = aux.astype(BF16)
        rest = (aux - high.astype(F32)).astype(BF16)
        is_rest = (lane >= experts_all) & (lane < 2 * experts_all)
        outs[1][:, MODEL_WIDTH:] = jnp.where(is_rest, rest, high)
        outs[2][...] = aux


def run_experts(place, x, dy, gates, zbias, sbias, mats, carried, shards, experts_all, rows_out, last):
    count, _, _, rows, _ = shards[0].shape
    first = carried is None
    acc_widths = (MODEL_WIDTH, MODEL_WIDTH, LANES, HIDDEN, 2 * HIDDEN)
    widths = (MODEL_WIDTH, MODEL_WIDTH + LANES if last else MODEL_WIDTH, *acc_widths[2:])
    dtypes = (BF16, BF16, F32, BF16, BF16)

    def tiled(width):
        return pl.BlockSpec((TILE, width), lambda t, place: (place[1] + t, 0))

    def out_tiled(width):
        return pl.BlockSpec((TILE, width), lambda t, _: (t, 0))

    in_widths = (MODEL_WIDTH, MODEL_WIDTH, LANES, 2 * HIDDEN, HIDDEN)
    specs = [tiled(w) for w in in_widths]
    specs += [pl.BlockSpec(m.shape, lambda t, _: (0, 0)) for m in mats]
    specs += [] if first else [out_tiled(w) for w in acc_widths]
    specs += [pl.BlockSpec(memory_space=pl.ANY)] * len(shards)
    copies = len(shards) * 2
    return pl.pallas_call(
        functools.partial(
            expert_kernel, len(shards), experts_all, first, last
        ),
        grid_spec=pltpu.PrefetchScalarGridSpec(
            num_scalar_prefetch=1,
            grid=(rows_out // TILE,),
            in_specs=specs,
            out_specs=[out_tiled(w) for w in widths],
            scratch_shapes=[
                pltpu.VMEM((count, 2, len(shards), 3, rows, HIDDEN), BF16),
                pltpu.VMEM((count, 3, len(shards), rows, HIDDEN), BF16),
                *[pltpu.VMEM((TILE, w), F32) for w in acc_widths],
                pltpu.SemaphoreType.DMA((count, copies)),
            ],
        ),
        out_shape=[jax.ShapeDtypeStruct((rows_out, w), t) for w, t in zip(widths, dtypes)],
        compiler_params=pltpu.CompilerParams(vmem_limit_bytes=60 * 2**20),
        cost_estimate=pl.CostEstimate(
            flops=12 * rows_out * MODEL_WIDTH * HIDDEN * count,
            bytes_accessed=rows_out * MODEL_WIDTH * 10,
            transcendentals=rows_out * HIDDEN * count,
        ),
    )(place, x, dy, gates, zbias, sbias, *mats, *(carried or ()), *shards)


def norm_backward(value_rows, inverse, gain_row, upstream):
    scaled = upstream * gain_row
    inner_mean = jnp.mean(value_rows * scaled, axis=-1, keepdims=True)
    return inverse * scaled - value_rows * (inverse * inverse * inverse) * inner_mean


def layout(lengths_row, prompt_len, total_len):
    ends = jnp.sum(jnp.tril(jnp.ones((lengths_row.shape[0],) * 2, jnp.int32)) * lengths_row, axis=1)
    starts = ends - lengths_row
    places = jnp.arange(total_len, dtype=jnp.int32)
    offset = places - prompt_len
    counted = jnp.sum((offset[:, None] >= ends[None, :]).astype(jnp.int32), axis=1)
    inside = offset >= 0
    segment = jnp.where(inside, counted, -1)
    picked = jnp.arange(lengths_row.shape[0], dtype=jnp.int32)[None, :] == counted[:, None]
    begin = jnp.sum(jnp.where(picked, starts[None, :], 0), axis=1)
    position = jnp.where(inside, prompt_len + offset - begin, places)
    return (segment, position)


def pad_lanes(x, at=0, width=LANES):
    return jnp.pad(x, ((0, 0), (at, width - at - x.shape[1])))


def gather_groups(x, n_dp, n_wt):
    row = jnp.stack([shift(x, "dp", n_dp, k) if k else x for k in range(n_dp)])
    return jnp.concatenate([shift(row, "wt", n_wt, b) if b else row for b in range(n_wt)])


def reduce_seq(flat, n_seq):
    rows, width = flat.shape
    return scatter_seq(flat.reshape(n_seq, rows // n_seq, width), n_seq)


def tagged(mine, index_now):
    return jnp.concatenate([mine, jnp.full((8, mine.shape[1]), index_now.astype(F32))], 0)


def by_adapter(everyone, names, n_seq, n_wt):
    share = ADAPTER_COUNT // n_wt
    part, width = everyone.shape[1:]
    first_row = lax.axis_index("wt") * share
    picks = (names[None, :] == first_row + jnp.arange(share)[:, None]).astype(F32)
    kept = jnp.sum(picks[:, :, None, None] * everyone[None].astype(F32), axis=1)
    pieces = seq_pieces(kept.reshape(share * part, width), n_seq)
    place = jnp.arange(n_seq)[None, :, None, None]
    full = sum(jnp.where(place == at, x.reshape(share, 1, part, width), 0.0) for at, x in pieces)
    return full.reshape(share, n_seq * part, width)


def shards(
    tokens,
    cotangent,
    routes,
    lengths,
    group_adapter_index,
    attention_norm_gain,
    query_weight,
    key_value_weight,
    output_weight,
    mixture_norm_gain,
    router_weight,
    expert_gate_up_weight,
    expert_down_weight,
    attention_first_factors,
    query_second_factor,
    key_value_second_factors,
    output_first_factor,
    output_second_factor,
    mixture_first_factors,
    router_second_factor,
    gate_up_second_factors,
    down_first_factor,
    down_second_factor,
):
    n_seq, n_dp, n_wt = (lax.axis_size(a) for a in ("seq", "dp", "wt"))
    seq, dp, wt = (lax.axis_index(a) for a in ("seq", "dp", "wt"))
    local = tokens.shape[1]
    total = local * n_seq
    prompt_len = max(PROMPT_LEAST, PROMPT_DEV * n_seq)
    exp_dev = expert_gate_up_weight.shape[0]
    experts_all = exp_dev * n_seq
    kv_local = KV_HEADS // n_seq
    group = HEADS // KV_HEADS
    q_width = MODEL_WIDTH // n_seq
    k_width = KEY_FEATURES // n_seq
    rank = ADAPTER_RANK
    index_now = group_adapter_index[0]

    def chosen(bank):
        return lax.dynamic_index_in_dim(bank, index_now, 0, keepdims=False)

    def own(x, size, axis=1, at=0):
        return lax.dynamic_slice_in_dim(x, at + seq * size, size, axis)

    attn_first = chosen(attention_first_factors)
    query_second = own(chosen(query_second_factor), q_width)
    kv_second = chosen(key_value_second_factors)
    out_first = chosen(output_first_factor)
    out_second = chosen(output_second_factor)
    mix_first = chosen(mixture_first_factors)
    router_second = chosen(router_second_factor)
    gate_up_second = chosen(gate_up_second_factors)
    down_first = chosen(down_first_factor)
    down_second = chosen(down_second_factor)

    def own_rows(x):
        return lax.dynamic_slice_in_dim(x, seq * local, local, 0)

    split = FIRST_EXPERTS
    tie = lax.optimization_barrier

    def across(x):
        return [shift(x, "dp", n_dp, k) for k in range(1, n_dp)]

    class Ring:
        def __init__(self, packed, begin):
            self.pieces, self.steps = [packed], 0
            self.came, self.moved = shift(begin, "wt", n_wt, 1), across(packed)

        def advance(self, gate=None):
            if self.steps == n_wt - 1:
                return
            self.steps += 1
            self.came, *self.moved, _ = tie((self.came, *self.moved, 0 if gate is None else gate))
            self.pieces += [*self.moved, self.came]
            self.moved = across(self.came)
            self.came = shift(self.came, "wt", n_wt, 1) if self.steps < n_wt - 1 else self.came

        def finish(self):
            while self.steps < n_wt - 1:
                self.advance()
            return self.pieces + self.moved

    order = [(0, 0)]
    for b in range(n_wt - 1):
        order += [(k, b) for k in range(1, n_dp)] + [(0, b + 1)]
    order += [(k, n_wt - 1) for k in range(1, n_dp)]
    ahead = pack_experts(expert_gate_up_weight[:split], expert_down_weight[:split])
    ahead = Ring(ahead, ahead)

    hidden = gather_seq(tokens[0], n_seq).reshape(total, MODEL_WIDTH)

    def gather_weights(x):
        return lax.all_gather(x, ("dp", "wt"), axis=0, tiled=True)

    mine = jnp.concatenate(
        [
            own(query_weight, q_width),
            own(key_value_weight, k_width),
            own(key_value_weight, k_width, at=KEY_FEATURES),
            pad_lanes(router_weight),
        ],
        axis=1,
    )
    gathered = gather_weights(mine)
    qkv_width = q_width + 2 * k_width
    qkv_weight = gathered[:, :qkv_width]
    router_full = gathered[:, qkv_width : qkv_width + experts_all]
    half = MODEL_WIDTH // 2
    core = seq % 2
    out_mine = gather_weights(lax.dynamic_slice_in_dim(output_weight, core * half, half, 1))
    out_other = swap_core(out_mine, n_seq)
    out_weight = jnp.where(
        core == 0,
        jnp.concatenate([out_mine, out_other], 1),
        jnp.concatenate([out_other, out_mine], 1),
    )

    gain_first = attention_norm_gain.astype(F32)
    gain_second = mixture_norm_gain.astype(F32)
    hidden_f = hidden.astype(F32)
    inverse_a = lax.rsqrt(jnp.mean(hidden_f * hidden_f, axis=-1, keepdims=True) + EPS)
    normed = (hidden_f * inverse_a * gain_first).astype(BF16)
    small_a = dot(normed, attn_first).astype(BF16)
    second = jnp.zeros((3 * rank, qkv_width), BF16)
    second = second.at[:rank, :q_width].set(query_second)
    second = second.at[rank : 2 * rank, q_width : q_width + k_width].set(own(kv_second[0], k_width))
    second = second.at[2 * rank :, q_width + k_width :].set(own(kv_second[1], k_width))
    qkv = dot(qkv_weight, normed, ((0,), (1,))) + dot(second, small_a, ((0,), (1,)))
    ahead.advance(normed)
    behind = pack_experts(expert_gate_up_weight[split:], expert_down_weight[split:])
    begin, _ = tie((behind, ahead.pieces[-1]))
    behind = Ring(behind, begin)
    segment, position = layout(lengths[0], prompt_len, total)
    freq = jnp.exp(jnp.arange(HEAD // 2, dtype=F32) * (-2.0 * math.log(10000.0) / HEAD))
    angle = freq[:, None] * position.astype(F32)[None, :]
    cosine, sine = jnp.cos(angle), jnp.sin(angle)

    def rotate(x, scale=1.0):
        x = x.reshape(-1, 2, HEAD // 2, total)
        a, b = x[:, 0], x[:, 1]
        x = jnp.concatenate([a * cosine - b * sine, b * cosine + a * sine], axis=1)
        return (x.astype(BF16) * jnp.asarray(scale, BF16)).reshape(-1, HEAD, total)

    qt = rotate(qkv[:q_width], HEAD**-0.5).reshape(kv_local, group, HEAD, total)
    kt = rotate(qkv[q_width : q_width + k_width])
    vt = qkv[q_width + k_width :].astype(BF16).reshape(kv_local, HEAD, total)
    ot, probs, inverse_l = attend(qt, kt, vt, segment, prompt_len, local)
    ahead.advance(ot)
    att = gather_seq(ot.reshape(q_width, total), n_seq).reshape(MODEL_WIDTH, total)

    behind.advance(att)
    ahead.advance(att)
    named = jnp.arange(LANES, dtype=jnp.int32)[None, None, :]
    mask = jnp.any(routes[0][:, :, None] == named, axis=1).astype(BF16)
    d_out = jnp.concatenate([cotangent[0], mask], axis=1)
    d_out, _ = lax.optimization_barrier((d_out, hidden))
    d_out = gather_seq(d_out, n_seq).reshape(total, MODEL_WIDTH + LANES)
    d_out_all = d_out[:, :MODEL_WIDTH]
    routed = d_out[:, MODEL_WIDTH : MODEL_WIDTH + experts_all] > 0.5

    small_o = dot_tn(att, out_first).astype(BF16)
    residual = hidden_f + dot_tn(att, out_weight) + dot(small_o, out_second)
    behind.advance(residual)
    inverse_m = lax.rsqrt(jnp.mean(residual * residual, axis=-1, keepdims=True) + EPS)
    normed_m = (residual * inverse_m * gain_second).astype(BF16)
    ahead = ahead.finish()
    mix_router = jnp.concatenate([mix_first, router_full], axis=1)
    states = dot(normed_m, mix_router)
    small_m = states[:, : 3 * rank].astype(BF16)
    logits = states[:, 3 * rank :] + dot(small_m[:, :rank], router_second)
    logits = jnp.where(routed, logits, NEG)
    peak = jnp.max(logits, axis=-1, keepdims=True)
    weights = jnp.where(routed, jnp.exp(logits - peak), 0.0)
    gating = weights / jnp.sum(weights, axis=-1, keepdims=True)

    d_rank = dot_nt(d_out_all, down_second).astype(BF16)
    gus = jnp.zeros((2 * rank, 2 * HIDDEN), BF16)
    gus = gus.at[:rank, :HIDDEN].set(gate_up_second[0])
    gus = gus.at[rank:, HIDDEN:].set(gate_up_second[1])
    mats = (pad_lanes(down_first, DOWN_AT), pad_lanes(gus.T, SMALL_AT))
    zbias = dot(small_m[:, rank:], gus).astype(BF16)
    sbias = dot_nt(d_rank, down_first).astype(BF16)
    gates = pad_lanes(gating)

    places = [(dp + n_dp - k) % n_dp * n_wt + (wt + n_wt - b) % n_wt for k, b in order]

    def place_of(expert, row):
        return jnp.stack([x.astype(jnp.int32) for x in (seq * exp_dev + expert, row, *places)])

    chip_rows = 2 * local
    firsts = []
    for k, chip in chip_turns(n_seq):
        firsts.append(
            list(run_experts(
                place_of(0, chip * (chip_rows // TILE)), normed_m, d_out_all, gates, zbias, sbias,
                mats, None, ahead, experts_all, chip_rows, False,
            ))
        )
        if len(firsts) == 1:
            behind.advance(firsts[0][2])
    behind = behind.finish()
    turns, arrived, waiting = [], [], None
    firsts[0][2], _ = tie((firsts[0][2], firsts[-1][2]))
    for (k, chip), carried in zip(chip_turns(n_seq), firsts):
        place = place_of(split, chip * (chip_rows // TILE))
        if waiting is not None:
            place, sent = tie((place, waiting[1].astype(BF16)))
            arrived.append(shift_chip(sent, n_seq, waiting[0]))
        parts = run_experts(
            place, normed_m, d_out_all, gates, zbias, sbias, mats, carried, behind,
            experts_all, chip_rows, True,
        )
        parts = list(parts)
        if arrived:
            arrived[-1], parts[1] = tie((arrived[-1], parts[1]))
        turns.append((k, chip, parts))
        waiting = (k, core_sum(parts[1].reshape(2, local, -1), n_seq))
    back_sum = waiting[1] + sum(x.astype(F32) for x in arrived)

    upstream = cotangent[0].astype(F32)
    residual_own = own_rows(residual)
    gating_own = own_rows(gating)
    small_m_own = own_rows(small_m)
    d_gating = (
        back_sum[:, MODEL_WIDTH : MODEL_WIDTH + experts_all]
        + back_sum[:, MODEL_WIDTH + experts_all : MODEL_WIDTH + 2 * experts_all]
    )
    d_logits = gating_own * (d_gating - jnp.sum(d_gating * gating_own, axis=-1, keepdims=True))
    d_logits_low = d_logits.astype(BF16)
    d_small_m = jnp.concatenate(
        [dot_nt(d_logits_low, router_second), back_sum[:, MODEL_WIDTH + SMALL_AT :]], axis=1
    ).astype(BF16)
    small_d = back_sum[:, MODEL_WIDTH + DOWN_AT : MODEL_WIDTH + DOWN_AT + rank].astype(BF16)
    d_normed_m = back_sum[:, :MODEL_WIDTH] + dot_nt(
        jnp.concatenate([d_small_m, d_logits_low], axis=1), mix_router
    )
    d_residual = upstream + norm_backward(
        residual_own, own_rows(inverse_m), gain_second, d_normed_m
    )
    d_branch = d_residual.astype(BF16)
    d_small_o = dot_nt(d_branch, out_second).astype(BF16)
    d_att = (dot_nt(out_weight, d_branch) + dot_nt(out_first, d_small_o)).astype(BF16)
    d_att = spread_seq(d_att.reshape(n_seq, q_width, local), n_seq)

    def of_chip(x, chip, axis=0):
        return lax.dynamic_slice_in_dim(x, chip * chip_rows, chip_rows, axis)

    grad_gu = sum(dot_tn(of_chip(small_m[:, rank:], chip), parts[4]) for _, chip, parts in turns)
    grad_down = sum(dot_tn(of_chip(d_rank, chip), parts[3]) for _, chip, parts in turns)
    att_own = lax.dynamic_slice_in_dim(att, seq * local, local, 1)
    early = jnp.concatenate(
        [
            dot(d_small_o, att_own, ((0,), (1,))),
            dot_tn(own_rows(small_o), d_branch),
            dot_tn(d_small_m, own_rows(normed_m)),
            dot_tn(small_d, cotangent[0]),
            jnp.concatenate([grad_gu[:rank, :HIDDEN], grad_gu[rank:, HIDDEN:], grad_down], axis=1),
            pad_lanes(dot_tn(small_m_own[:, :rank], d_logits_low), width=MODEL_WIDTH),
        ],
        axis=0,
    )
    early = reduce_seq(early, n_seq)
    parts_out = [core_sum(parts[0].reshape(2, local, -1), n_seq) for _, _, parts in turns]
    early, d_att, *parts_sent = tie((early, d_att, *[x.astype(BF16) for x in parts_out[:-1]]))
    early = lax.all_gather(tagged(early, index_now), ("dp", "wt"), axis=0)
    sent = [shift_chip(x, n_seq, k) for x, (k, _, _) in zip(parts_sent, turns)]
    dqt, dkt, dvt = attend_back(
        qt, kt, vt, ot, d_att.reshape(n_seq, kv_local, group, HEAD, local), probs, inverse_l,
        cosine, sine,
    )
    dqt, *sent = tie((dqt, *sent))
    output_rows = residual_own + dot(small_d, down_second) + parts_out[-1]
    output_rows = output_rows + sum(x.astype(F32) for x in sent)

    d_qkv = jnp.concatenate(
        [dqt.reshape(q_width, total), dkt.reshape(k_width, total), dvt.reshape(k_width, total)], 0
    )
    d_small_a = dot(d_qkv, second, ((0,), (1,))).astype(BF16)
    grad_second = dot(small_a, d_qkv, ((0,), (1,)))

    def spread(x, width, full):
        return lax.dynamic_update_slice_in_dim(
            jnp.zeros((x.shape[0], full), F32), x, seq * width, 1
        )

    late = jnp.concatenate(
        [
            dot_tn(d_small_a, normed),
            spread(grad_second[:rank, :q_width], q_width, MODEL_WIDTH),
            jnp.concatenate(
                [
                    spread(grad_second[rank : 2 * rank, q_width : q_width + k_width], k_width, KEY_FEATURES),
                    spread(grad_second[2 * rank :, q_width + k_width :], k_width, KEY_FEATURES),
                    jnp.zeros((rank, MODEL_WIDTH - 2 * KEY_FEATURES), F32),
                ],
                axis=1,
            ),
        ],
        axis=0,
    )
    late = reduce_seq(late, n_seq)
    d_normed = None
    for k, chip in chip_turns(n_seq):
        part = dot(of_chip(d_qkv, chip, 1), qkv_weight, ((0,), (1,)))
        part = part + dot_nt(of_chip(d_small_a, chip), attn_first)
        part = core_sum(part.astype(BF16).reshape(2, local, MODEL_WIDTH), n_seq)
        if k:
            late, part = tie((late, part.astype(BF16)))
            part = shift_chip(part, n_seq, k).astype(F32)
        d_normed = part if d_normed is None else d_normed + part
    input_grad = d_residual + norm_backward(
        tokens[0].astype(F32), own_rows(inverse_a), gain_first, d_normed
    )
    names = early[:, -1, 0].astype(jnp.int32)
    early = by_adapter(early[:, :-8], names, n_seq, n_wt)
    turned = jnp.stack(
        [
            (dp + n_dp - k) % n_dp * n_wt + (wt + n_wt - b) % n_wt
            for b in range(n_wt) for k in range(n_dp)
        ]
    )
    late = by_adapter(gather_groups(late.astype(BF16), n_dp, n_wt), names[turned], n_seq, n_wt)

    def flip(x):
        return jnp.swapaxes(x, 1, 2)

    def at(flat, row, count, lo=0, hi=MODEL_WIDTH):
        return flat[:, row : row + count, lo:hi]

    low = 6 * rank
    return (
        output_rows[None].astype(BF16),
        input_grad[None],
        flip(at(late, 0, 3 * rank)),
        at(late, 3 * rank, rank),
        jnp.stack(
            [at(late, 4 * rank, rank, m, m + KEY_FEATURES) for m in (0, KEY_FEATURES)], axis=1
        ),
        flip(at(early, 0, rank)),
        at(early, rank, rank),
        flip(at(early, 2 * rank, 3 * rank)),
        at(early, low + rank, rank, 0, experts_all),
        jnp.stack([at(early, low, rank, m, m + HIDDEN) for m in (0, HIDDEN)], axis=1),
        flip(at(early, low, rank, 2 * HIDDEN, 3 * HIDDEN)),
        at(early, 5 * rank, rank),
    )


def solution(mesh):
    split = P(("dp", "wt"), "seq", None)
    rows = P(("dp", "wt"), None)
    bank = P("wt", None, None)
    placed = (
        split, split, split, rows, P(("dp", "wt")), P(), rows, rows, rows, P(), rows,
        P("seq", ("dp", "wt"), None), P("seq", ("dp", "wt"), None),
    ) + (P(),) * 10
    wide = P("wt", None, None, None)
    return jax.shard_map(
        shards,
        mesh=mesh,
        in_specs=placed,
        out_specs=(split, split, bank, bank, wide, bank, bank, bank, bank, wide, bank, bank),
        check_vma=False,
    )
```

```python
import functools
import math

import jax
import jax.numpy as jnp
from jax import lax
from jax.experimental import pallas as pl
from jax.experimental.pallas import tpu as pltpu
from jax.sharding import PartitionSpec as P

MODEL_WIDTH = 1536
HEADS = 24
KV_HEADS = 8
HEAD = 64
HIDDEN = 512
ADAPTER_RANK = 16
ADAPTER_COUNT = 8
PROMPT_LEAST = 1024
PROMPT_DEV = 128
KEY_FEATURES = 512
LANES = 128
SMALL_AT = 96

EPS = 1e-05
NEG = -1e30
F32 = jnp.float32
BF16 = jnp.bfloat16
FIRST_EXPERTS = 3
HOLD = 1
TILE = 256
DOWN_AT = 80


def dot(a, b, dims=((1,), (0,))):
    return lax.dot_general(a, b, (dims, ((), ())), preferred_element_type=F32)


def dot_nt(a, b):
    return dot(a, b, ((1,), (1,)))


def dot_tn(a, b):
    return dot(a, b, ((0,), (0,)))


def swap_core(x, n_seq):
    return lax.ppermute(x, "seq", [(i, i ^ 1) for i in range(n_seq)])


def shift_chip(x, n_seq, k):
    n_y = n_seq // 2
    pairs = [(y * 2 + c, (y + k) % n_y * 2 + c) for y in range(n_y) for c in range(2)]
    return lax.ppermute(x, "seq", pairs)


def seq_pieces(x, n_seq):
    n_y = n_seq // 2
    me = lax.axis_index("seq")
    y, c = me // 2, me % 2
    far = [shift_chip(x, n_seq, k) for k in range(1, n_y)]
    pieces = [(me, x), (me ^ 1, swap_core(x, n_seq))]
    for k, piece in enumerate(far, 1):
        chip = (y + n_y - k) % n_y * 2
        pieces += [(chip + c, piece), (chip + 1 - c, swap_core(piece, n_seq))]
    return pieces


def gather_seq(x, n_seq):
    out = jnp.zeros((n_seq,) + x.shape, x.dtype)
    for at, piece in seq_pieces(x, n_seq):
        out = lax.dynamic_update_slice_in_dim(out, piece[None], at, 0)
    return out


def core_sum(x, n_seq):
    c = lax.axis_index("seq") % 2
    got = swap_core(lax.dynamic_index_in_dim(x, 1 - c, 0, keepdims=False), n_seq)
    kept = lax.dynamic_index_in_dim(x, c, 0, keepdims=False)
    return kept.astype(F32) + got.astype(F32)


def scatter_piece(x, n_seq, k):
    both = core_sum(x, n_seq)
    return shift_chip(both.astype(x.dtype), n_seq, k).astype(F32) if k else both


def chip_turns(n_seq):
    n_y = n_seq // 2
    y = lax.axis_index("seq") // 2
    return [(k, (y + k) % n_y) for k in [*range(1, n_y), 0]]


def scatter_seq(x, n_seq):
    x = x.reshape((n_seq // 2, 2) + x.shape[1:])
    return sum(
        scatter_piece(lax.dynamic_index_in_dim(x, chip, 0, keepdims=False), n_seq, k)
        for k, chip in chip_turns(n_seq)
    )


def spread_seq(x, n_seq):
    n_y = n_seq // 2
    me = lax.axis_index("seq")
    y, c = me // 2, me % 2
    x = x.reshape((n_y, 2) + x.shape[1:])
    out = jnp.zeros((n_seq,) + x.shape[2:], x.dtype)
    for k, chip in chip_turns(n_seq):
        pair = lax.dynamic_index_in_dim(x, chip, 0, keepdims=False)
        if k:
            pair = shift_chip(pair, n_seq, k)
        other = swap_core(lax.dynamic_index_in_dim(pair, 1 - c, 0, keepdims=False), n_seq)
        same = lax.dynamic_index_in_dim(pair, c, 0, keepdims=False)
        at = (y + n_y - k) % n_y * 2
        out = lax.dynamic_update_slice_in_dim(out, same[None], at + c, 0)
        out = lax.dynamic_update_slice_in_dim(out, other[None], at + 1 - c, 0)
    return out


def shift(x, axis, count, k):
    return lax.ppermute(x, axis, [(i, (i + k) % count) for i in range(count)])


def column_fold(x, op):
    rows, width = x.shape
    return op(x.reshape(rows // 8, 8, width), axis=0)


def attend_kernel(
    prompt_blocks, q_ref, k_ref, v_ref, segq_ref, segk_ref, o_ref, p_ref, inv_ref, krow, scores
):
    i = pl.program_id(1)
    group, qb = q_ref.shape[1], q_ref.shape[3]
    width = group * qb

    @pl.when(i == 0)
    def _():
        krow[...] = k_ref[0].astype(F32).T.astype(BF16)

    q = jnp.concatenate([q_ref[0, h] for h in range(group)], axis=1)
    segq = jnp.concatenate([segq_ref[...]] * group, axis=1)
    placeq = i * qb + lax.broadcasted_iota(jnp.int32, (1, width), 1) % qb

    def score(j, peak, masked):
        rows = pl.ds(pl.multiple_of(j * qb, qb), qb)
        s = dot(krow[rows, :], q)
        if masked:
            segk = segk_ref[rows, :]
            placek = j * qb + lax.broadcasted_iota(jnp.int32, (qb, 1), 0)
            keep = (placek <= placeq) & ((segk < 0) | (segk == segq))
            s = jnp.where(keep, s, NEG)
        scores[rows, :] = s
        return jnp.maximum(peak, column_fold(s, jnp.max))

    free = jnp.minimum(i, prompt_blocks)
    peak = jnp.full((8, width), NEG, F32)
    peak = lax.fori_loop(0, free, lambda j, m: score(j, m, False), peak)
    peak = lax.fori_loop(free, i + 1, lambda j, m: score(j, m, True), peak)
    peak = jnp.max(peak, axis=0, keepdims=True)

    def weigh(j, carry):
        total, acc = carry
        rows = pl.ds(pl.multiple_of(j * qb, qb), qb)
        p = jnp.exp(scores[rows, :] - peak)
        low = p.astype(BF16)
        p_ref[0, 0, rows, :] = low
        return total + column_fold(p, jnp.sum), acc + dot(v_ref[0, :, rows], low)

    total, acc = lax.fori_loop(
        0, i + 1, weigh, (jnp.zeros((8, width), F32), jnp.zeros((HEAD, width), F32))
    )
    inverse = 1.0 / jnp.sum(total, axis=0, keepdims=True)
    inv_ref[0, 0] = inverse
    out = (acc * inverse).astype(BF16)
    for h in range(group):
        o_ref[0, h] = out[:, h * qb : (h + 1) * qb]


def attend(qt, kt, vt, segment, prompt_len, block):
    kv, group, _, total = qt.shape
    blocks = total // block
    width = group * block
    pairs = kv * group * total * total // 2
    return pl.pallas_call(
        functools.partial(attend_kernel, prompt_len // block),
        grid=(kv, blocks),
        in_specs=[
            pl.BlockSpec((1, group, HEAD, block), lambda b, i: (b, 0, 0, i)),
            pl.BlockSpec((1, HEAD, total), lambda b, i: (b, 0, 0)),
            pl.BlockSpec((1, HEAD, total), lambda b, i: (b, 0, 0)),
            pl.BlockSpec((1, block), lambda b, i: (0, i)),
            pl.BlockSpec((total, 1), lambda b, i: (0, 0)),
        ],
        out_specs=[
            pl.BlockSpec((1, group, HEAD, block), lambda b, i: (b, 0, 0, i)),
            pl.BlockSpec((1, 1, total, width), lambda b, i: (b, i, 0, 0)),
            pl.BlockSpec((1, 1, 1, width), lambda b, i: (b, i, 0, 0)),
        ],
        out_shape=[
            jax.ShapeDtypeStruct(qt.shape, BF16),
            jax.ShapeDtypeStruct((kv, blocks, total, width), BF16),
            jax.ShapeDtypeStruct((kv, blocks, 1, width), F32),
        ],
        scratch_shapes=[pltpu.VMEM((total, HEAD), BF16), pltpu.VMEM((total, width), F32)],
        compiler_params=pltpu.CompilerParams(vmem_limit_bytes=40 * 2**20),
        cost_estimate=pl.CostEstimate(
            flops=pairs * HEAD * 4, bytes_accessed=pairs * 4, transcendentals=pairs
        ),
    )(qt, kt, vt, segment[None, :], segment[:, None])


def unrotate(grad, cosine, sine):
    half = HEAD // 2
    first, second = grad[:half], grad[half:]
    return jnp.concatenate(
        [first * cosine + second * sine, second * cosine - first * sine], axis=0
    )


def attend_back_kernel(
    q_ref, k_ref, v_ref, o_ref, do_ref, p_ref, inv_ref, cosq_ref, sinq_ref, cos_ref, sin_ref,
    dq_ref, dk_ref, dv_ref, vrow, dk_acc, dv_acc,
):
    i = pl.program_id(1)
    group, qb = q_ref.shape[1], q_ref.shape[3]
    width = group * qb

    @pl.when(i == 0)
    def _():
        vrow[...] = v_ref[0].astype(F32).T.astype(BF16)
        dk_acc[...] = jnp.zeros_like(dk_acc)
        dv_acc[...] = jnp.zeros_like(dv_acc)

    def side(ref, *at):
        return jnp.concatenate([ref[(0, *at, h)].astype(F32) for h in range(group)], axis=1)

    do = side(do_ref, 0) * inv_ref[0, 0]
    centre = jnp.sum(side(o_ref) * do, axis=0, keepdims=True)
    do_low = do.astype(BF16)
    do_rows = do.T.astype(BF16)
    q_rows = side(q_ref).T.astype(BF16)

    def step(j, acc):
        rows = pl.ds(pl.multiple_of(j * qb, qb), qb)
        p = p_ref[0, 0, rows, :]
        dp = dot(vrow[rows, :], do_low)
        ds = (p.astype(F32) * (dp - centre)).astype(BF16)
        dk_acc[rows, :] += dot(ds, q_rows)
        dv_acc[rows, :] += dot(p, do_rows)
        return acc + dot(k_ref[0, :, rows], ds)

    dq = lax.fori_loop(0, i + 1, step, jnp.zeros((HEAD, width), F32)) * HEAD**-0.5
    for h in range(group):
        part = dq[:, h * qb : (h + 1) * qb]
        dq_ref[0, h] = unrotate(part, cosq_ref[...], sinq_ref[...]).astype(BF16)

    @pl.when(i == pl.num_programs(1) - 1)
    def _():
        dk_ref[0] = unrotate(dk_acc[...].T, cos_ref[...], sin_ref[...]).astype(BF16)
        dv_ref[0] = dv_acc[...].T.astype(BF16)


def attend_back(qt, kt, vt, ot, do, p, inverse, cosine, sine):
    kv, group, _, total = qt.shape
    blocks, block = do.shape[0], do.shape[-1]
    width = group * block
    pairs = kv * group * total * total // 2
    q_spec = pl.BlockSpec((1, group, HEAD, block), lambda b, i: (b, 0, 0, i))
    k_spec = pl.BlockSpec((1, HEAD, total), lambda b, i: (b, 0, 0))
    return pl.pallas_call(
        attend_back_kernel,
        grid=(kv, blocks),
        in_specs=[
            q_spec, k_spec, k_spec, q_spec,
            pl.BlockSpec((1, 1, group, HEAD, block), lambda b, i: (i, b, 0, 0, 0)),
            pl.BlockSpec((1, 1, total, width), lambda b, i: (b, i, 0, 0)),
            pl.BlockSpec((1, 1, 1, width), lambda b, i: (b, i, 0, 0)),
            pl.BlockSpec((HEAD // 2, block), lambda b, i: (0, i)),
            pl.BlockSpec((HEAD // 2, block), lambda b, i: (0, i)),
            pl.BlockSpec((HEAD // 2, total), lambda b, i: (0, 0)),
            pl.BlockSpec((HEAD // 2, total), lambda b, i: (0, 0)),
        ],
        out_specs=[q_spec, k_spec, k_spec],
        out_shape=[
            jax.ShapeDtypeStruct(qt.shape, BF16),
            jax.ShapeDtypeStruct(kt.shape, BF16),
            jax.ShapeDtypeStruct(vt.shape, BF16),
        ],
        scratch_shapes=[
            pltpu.VMEM((total, HEAD), BF16),
            pltpu.VMEM((total, HEAD), F32),
            pltpu.VMEM((total, HEAD), F32),
        ],
        compiler_params=pltpu.CompilerParams(vmem_limit_bytes=40 * 2**20),
        cost_estimate=pl.CostEstimate(
            flops=pairs * HEAD * 8, bytes_accessed=pairs * 4, transcendentals=0
        ),
    )(qt, kt, vt, ot, do, p, inverse, cosine, sine, cosine, sine)


def pack_experts(gate_up, down):
    count, _, _ = gate_up.shape
    rows = down.shape[1]
    parts = [gate_up[..., :HIDDEN], gate_up[..., HIDDEN:]]
    parts += [down[..., m : m + HIDDEN] for m in range(0, MODEL_WIDTH, HIDDEN)]
    return jnp.concatenate(parts, axis=1).reshape(count, 3, 3, rows, HIDDEN)


def expert_kernel(
    shards_count, experts_all, first, last, place_ref, x_ref, dy_ref, gate_ref,
    zbias_ref, sbias_ref, dfa_ref, back_ref, *refs,
):
    refs = list(refs)
    carried = [None] * 5 if first else [refs.pop(0) for _ in range(5)]
    shards = [refs.pop(0) for _ in range(shards_count)]
    outs = [refs.pop(0) for _ in range(5)]
    w_up, w_down, *accs, sem = refs
    count = w_up.shape[0]
    tile = x_ref.shape[0]

    def copies(e):
        pairs = []
        for b, shard in enumerate(shards):
            pairs.append((shard.at[e, pl.ds(0, 2)], w_up.at[e, :, place_ref[2 + b]]))
            pairs.append((shard.at[e, 2], w_down.at[e, :, place_ref[2 + b]]))
        return [pltpu.make_async_copy(a, b, sem.at[e, n]) for n, (a, b) in enumerate(pairs)]

    lane = lax.broadcasted_iota(jnp.int32, (tile, LANES), 1)

    def add(n, e, value):
        base = carried[n] if e == 0 else accs[n]
        if base is not None:
            value = base[...].astype(F32) + value
        if e < count - 1:
            accs[n][...] = value
        elif n == 2 and last:
            accs[n][...] = value
        elif n == 1 and last:
            outs[n][:, :MODEL_WIDTH] = value.astype(outs[n].dtype)
        else:
            outs[n][...] = value.astype(outs[n].dtype)

    def step(e):
        name = place_ref[0] + e
        up_weight = jnp.concatenate(
            [w_up[e, m].reshape(MODEL_WIDTH, HIDDEN) for m in range(2)], axis=1
        )
        down_weight = jnp.concatenate(
            [w_down[e, m].reshape(HIDDEN, HIDDEN) for m in range(MODEL_WIDTH // HIDDEN)], axis=1
        )
        both = dot(x_ref[...], up_weight) + zbias_ref[...]
        gate_in, up = both[:, :HIDDEN], both[:, HIDDEN:]
        sigma = jax.nn.sigmoid(gate_in)
        silu = gate_in * sigma
        inner = silu * up
        d_down = dot_nt(dy_ref[...], down_weight) + sbias_ref[...]
        d_gating = jnp.sum(inner * d_down, axis=1, keepdims=True)
        gating = jnp.sum(jnp.where(lane == name, gate_ref[...], 0.0), axis=1, keepdims=True)
        add(2, e, jnp.where((lane == name) | (lane == name + experts_all), d_gating, 0.0))
        gated = gating * inner
        add(3, e, gated)
        add(0, e, dot(gated.astype(BF16), down_weight))
        d_inner = gating * d_down
        d_gate = d_inner * up * (sigma + silu * (1.0 - sigma))
        d_both = jnp.concatenate([d_gate, d_inner * silu], axis=1)
        add(4, e, d_both)
        add(1, e, dot_nt(d_both.astype(BF16), up_weight))

    @pl.when(pl.program_id(0) == 0)
    def _():
        for e in range(count):
            for copy in copies(e):
                copy.start()
        for e in range(count):
            for copy in copies(e):
                copy.wait()
            step(e)

    @pl.when(pl.program_id(0) > 0)
    def _():
        for e in range(count):
            step(e)

    if last:
        aux = accs[2][...] + dot(outs[3][...], dfa_ref[...]) + dot(outs[4][...], back_ref[...])
        high = aux.astype(BF16)
        rest = (aux - high.astype(F32)).astype(BF16)
        is_rest = (lane >= experts_all) & (lane < 2 * experts_all)
        outs[1][:, MODEL_WIDTH:] = jnp.where(is_rest, rest, high)
        outs[2][...] = aux


def run_experts(place, x, dy, gates, zbias, sbias, mats, carried, shards, experts_all, rows_out, last):
    count, _, _, rows, _ = shards[0].shape
    first = carried is None
    acc_widths = (MODEL_WIDTH, MODEL_WIDTH, LANES, HIDDEN, 2 * HIDDEN)
    widths = (MODEL_WIDTH, MODEL_WIDTH + LANES if last else MODEL_WIDTH, *acc_widths[2:])
    dtypes = (BF16, BF16, F32, BF16, BF16)

    def tiled(width):
        return pl.BlockSpec((TILE, width), lambda t, place: (place[1] + t, 0))

    def out_tiled(width):
        return pl.BlockSpec((TILE, width), lambda t, _: (t, 0))

    in_widths = (MODEL_WIDTH, MODEL_WIDTH, LANES, 2 * HIDDEN, HIDDEN)
    specs = [tiled(w) for w in in_widths]
    specs += [pl.BlockSpec(m.shape, lambda t, _: (0, 0)) for m in mats]
    specs += [] if first else [out_tiled(w) for w in acc_widths]
    specs += [pl.BlockSpec(memory_space=pl.ANY)] * len(shards)
    copies = len(shards) * 2
    return pl.pallas_call(
        functools.partial(
            expert_kernel, len(shards), experts_all, first, last
        ),
        grid_spec=pltpu.PrefetchScalarGridSpec(
            num_scalar_prefetch=1,
            grid=(rows_out // TILE,),
            in_specs=specs,
            out_specs=[out_tiled(w) for w in widths],
            scratch_shapes=[
                pltpu.VMEM((count, 2, len(shards), 3, rows, HIDDEN), BF16),
                pltpu.VMEM((count, 3, len(shards), rows, HIDDEN), BF16),
                *[pltpu.VMEM((TILE, w), F32) for w in acc_widths],
                pltpu.SemaphoreType.DMA((count, copies)),
            ],
        ),
        out_shape=[jax.ShapeDtypeStruct((rows_out, w), t) for w, t in zip(widths, dtypes)],
        compiler_params=pltpu.CompilerParams(vmem_limit_bytes=60 * 2**20),
        cost_estimate=pl.CostEstimate(
            flops=12 * rows_out * MODEL_WIDTH * HIDDEN * count,
            bytes_accessed=rows_out * MODEL_WIDTH * 10,
            transcendentals=rows_out * HIDDEN * count,
        ),
    )(place, x, dy, gates, zbias, sbias, *mats, *(carried or ()), *shards)


def norm_backward(value_rows, inverse, gain_row, upstream):
    scaled = upstream * gain_row
    inner_mean = jnp.mean(value_rows * scaled, axis=-1, keepdims=True)
    return inverse * scaled - value_rows * (inverse * inverse * inverse) * inner_mean


def layout(lengths_row, prompt_len, total_len):
    ends = jnp.sum(jnp.tril(jnp.ones((lengths_row.shape[0],) * 2, jnp.int32)) * lengths_row, axis=1)
    starts = ends - lengths_row
    places = jnp.arange(total_len, dtype=jnp.int32)
    offset = places - prompt_len
    counted = jnp.sum((offset[:, None] >= ends[None, :]).astype(jnp.int32), axis=1)
    inside = offset >= 0
    segment = jnp.where(inside, counted, -1)
    picked = jnp.arange(lengths_row.shape[0], dtype=jnp.int32)[None, :] == counted[:, None]
    begin = jnp.sum(jnp.where(picked, starts[None, :], 0), axis=1)
    position = jnp.where(inside, prompt_len + offset - begin, places)
    return (segment, position)


def pad_lanes(x, at=0, width=LANES):
    return jnp.pad(x, ((0, 0), (at, width - at - x.shape[1])))


def gather_groups(x, n_dp, n_wt):
    row = jnp.stack([shift(x, "dp", n_dp, k) if k else x for k in range(n_dp)])
    return jnp.concatenate([shift(row, "wt", n_wt, b) if b else row for b in range(n_wt)])


def reduce_seq(flat, n_seq):
    rows, width = flat.shape
    return scatter_seq(flat.reshape(n_seq, rows // n_seq, width), n_seq)


def tagged(mine, index_now):
    return jnp.concatenate([mine, jnp.full((8, mine.shape[1]), index_now.astype(F32))], 0)


def by_adapter(everyone, names, n_seq, n_wt):
    share = ADAPTER_COUNT // n_wt
    part, width = everyone.shape[1:]
    first_row = lax.axis_index("wt") * share
    picks = (names[None, :] == first_row + jnp.arange(share)[:, None]).astype(F32)
    kept = jnp.sum(picks[:, :, None, None] * everyone[None].astype(F32), axis=1)
    pieces = seq_pieces(kept.reshape(share * part, width), n_seq)
    stacked = jnp.stack([x.reshape(share, part, width) for _, x in pieces])
    me, n_y = lax.axis_index("seq"), n_seq // 2
    blocks = []
    for j in range(n_seq):
        turn = (me // 2 + n_y - j // 2) % n_y * 2 + (me + j) % 2
        blocks.append(lax.dynamic_index_in_dim(stacked, turn, 0, keepdims=False))
    return jnp.concatenate(blocks, axis=1)


def shards(
    tokens,
    cotangent,
    routes,
    lengths,
    group_adapter_index,
    attention_norm_gain,
    query_weight,
    key_value_weight,
    output_weight,
    mixture_norm_gain,
    router_weight,
    expert_gate_up_weight,
    expert_down_weight,
    attention_first_factors,
    query_second_factor,
    key_value_second_factors,
    output_first_factor,
    output_second_factor,
    mixture_first_factors,
    router_second_factor,
    gate_up_second_factors,
    down_first_factor,
    down_second_factor,
):
    n_seq, n_dp, n_wt = (lax.axis_size(a) for a in ("seq", "dp", "wt"))
    seq, dp, wt = (lax.axis_index(a) for a in ("seq", "dp", "wt"))
    local = tokens.shape[1]
    total = local * n_seq
    prompt_len = max(PROMPT_LEAST, PROMPT_DEV * n_seq)
    exp_dev = expert_gate_up_weight.shape[0]
    experts_all = exp_dev * n_seq
    kv_local = KV_HEADS // n_seq
    group = HEADS // KV_HEADS
    q_width = MODEL_WIDTH // n_seq
    k_width = KEY_FEATURES // n_seq
    rank = ADAPTER_RANK
    index_now = group_adapter_index[0]

    def chosen(bank):
        return lax.dynamic_index_in_dim(bank, index_now, 0, keepdims=False)

    def own(x, size, axis=1, at=0):
        return lax.dynamic_slice_in_dim(x, at + seq * size, size, axis)

    attn_first = chosen(attention_first_factors)
    query_second = own(chosen(query_second_factor), q_width)
    kv_second = chosen(key_value_second_factors)
    out_first = chosen(output_first_factor)
    out_second = chosen(output_second_factor)
    mix_first = chosen(mixture_first_factors)
    router_second = chosen(router_second_factor)
    gate_up_second = chosen(gate_up_second_factors)
    down_first = chosen(down_first_factor)
    down_second = chosen(down_second_factor)

    def own_rows(x):
        return lax.dynamic_slice_in_dim(x, seq * local, local, 0)

    split = FIRST_EXPERTS
    tie = lax.optimization_barrier

    def across(x):
        return [shift(x, "dp", n_dp, k) for k in range(1, n_dp)]

    class Ring:
        def __init__(self, packed, begin):
            self.pieces, self.steps = [packed], 0
            self.came, self.moved = shift(begin, "wt", n_wt, 1), across(packed)

        def advance(self, gate=None):
            if self.steps == n_wt - 1:
                return
            self.steps += 1
            self.came, *self.moved, _ = tie((self.came, *self.moved, 0 if gate is None else gate))
            self.pieces += [*self.moved, self.came]
            self.moved = across(self.came)
            self.came = shift(self.came, "wt", n_wt, 1) if self.steps < n_wt - 1 else self.came

        def finish(self):
            while self.steps < n_wt - 1:
                self.advance()
            return self.pieces + self.moved

    order = [(0, 0)]
    for b in range(n_wt - 1):
        order += [(k, b) for k in range(1, n_dp)] + [(0, b + 1)]
    order += [(k, n_wt - 1) for k in range(1, n_dp)]
    ahead = pack_experts(expert_gate_up_weight[:split], expert_down_weight[:split])
    ahead = Ring(ahead, ahead)

    hidden = gather_seq(tokens[0], n_seq).reshape(total, MODEL_WIDTH)

    def gather_weights(x):
        return lax.all_gather(x, ("dp", "wt"), axis=0, tiled=True)

    mine = jnp.concatenate(
        [
            own(query_weight, q_width),
            own(key_value_weight, k_width),
            own(key_value_weight, k_width, at=KEY_FEATURES),
            pad_lanes(router_weight),
        ],
        axis=1,
    )
    gathered = gather_weights(mine)
    qkv_width = q_width + 2 * k_width
    qkv_weight = gathered[:, :qkv_width]
    router_full = gathered[:, qkv_width : qkv_width + experts_all]
    half = MODEL_WIDTH // 2
    core = seq % 2
    out_mine = gather_weights(lax.dynamic_slice_in_dim(output_weight, core * half, half, 1))
    out_other = swap_core(out_mine, n_seq)
    out_weight = jnp.where(
        core == 0,
        jnp.concatenate([out_mine, out_other], 1),
        jnp.concatenate([out_other, out_mine], 1),
    )

    gain_first = attention_norm_gain.astype(F32)
    gain_second = mixture_norm_gain.astype(F32)
    hidden_f = hidden.astype(F32)
    inverse_a = lax.rsqrt(jnp.mean(hidden_f * hidden_f, axis=-1, keepdims=True) + EPS)
    normed = (hidden_f * inverse_a * gain_first).astype(BF16)
    small_a = dot(normed, attn_first).astype(BF16)
    second = jnp.zeros((3 * rank, qkv_width), BF16)
    second = second.at[:rank, :q_width].set(query_second)
    second = second.at[rank : 2 * rank, q_width : q_width + k_width].set(own(kv_second[0], k_width))
    second = second.at[2 * rank :, q_width + k_width :].set(own(kv_second[1], k_width))
    qkv = dot(qkv_weight, normed, ((0,), (1,))) + dot(second, small_a, ((0,), (1,)))
    ahead.advance(normed)
    behind = pack_experts(expert_gate_up_weight[split:], expert_down_weight[split:])
    begin, _ = tie((behind, ahead.pieces[-1]))
    behind = Ring(behind, begin)
    segment, position = layout(lengths[0], prompt_len, total)
    freq = jnp.exp(jnp.arange(HEAD // 2, dtype=F32) * (-2.0 * math.log(10000.0) / HEAD))
    angle = freq[:, None] * position.astype(F32)[None, :]
    cosine, sine = jnp.cos(angle), jnp.sin(angle)

    def rotate(x, scale=1.0):
        x = x.reshape(-1, 2, HEAD // 2, total)
        a, b = x[:, 0], x[:, 1]
        x = jnp.concatenate([a * cosine - b * sine, b * cosine + a * sine], axis=1)
        return (x.astype(BF16) * jnp.asarray(scale, BF16)).reshape(-1, HEAD, total)

    qt = rotate(qkv[:q_width], HEAD**-0.5).reshape(kv_local, group, HEAD, total)
    kt = rotate(qkv[q_width : q_width + k_width])
    vt = qkv[q_width + k_width :].astype(BF16).reshape(kv_local, HEAD, total)
    ot, probs, inverse_l = attend(qt, kt, vt, segment, prompt_len, local)
    ahead.advance(ot)
    att = gather_seq(ot.reshape(q_width, total), n_seq).reshape(MODEL_WIDTH, total)

    behind.advance(att)
    ahead.advance(att)
    named = jnp.arange(LANES, dtype=jnp.int32)[None, None, :]
    mask = jnp.any(routes[0][:, :, None] == named, axis=1).astype(BF16)
    d_out = jnp.concatenate([cotangent[0], mask], axis=1)
    d_out, _ = lax.optimization_barrier((d_out, hidden))
    d_out = gather_seq(d_out, n_seq).reshape(total, MODEL_WIDTH + LANES)
    d_out_all = d_out[:, :MODEL_WIDTH]
    routed = d_out[:, MODEL_WIDTH : MODEL_WIDTH + experts_all] > 0.5

    small_o = dot_tn(att, out_first).astype(BF16)
    residual = hidden_f + dot_tn(att, out_weight) + dot(small_o, out_second)
    behind.advance(residual)
    inverse_m = lax.rsqrt(jnp.mean(residual * residual, axis=-1, keepdims=True) + EPS)
    normed_m = (residual * inverse_m * gain_second).astype(BF16)
    ahead = ahead.finish()
    mix_router = jnp.concatenate([mix_first, router_full], axis=1)
    states = dot(normed_m, mix_router)
    small_m = states[:, : 3 * rank].astype(BF16)
    logits = states[:, 3 * rank :] + dot(small_m[:, :rank], router_second)
    logits = jnp.where(routed, logits, NEG)
    peak = jnp.max(logits, axis=-1, keepdims=True)
    weights = jnp.where(routed, jnp.exp(logits - peak), 0.0)
    gating = weights / jnp.sum(weights, axis=-1, keepdims=True)

    d_rank = dot_nt(d_out_all, down_second).astype(BF16)
    gus = jnp.zeros((2 * rank, 2 * HIDDEN), BF16)
    gus = gus.at[:rank, :HIDDEN].set(gate_up_second[0])
    gus = gus.at[rank:, HIDDEN:].set(gate_up_second[1])
    mats = (pad_lanes(down_first, DOWN_AT), pad_lanes(gus.T, SMALL_AT))
    zbias = dot(small_m[:, rank:], gus).astype(BF16)
    sbias = dot_nt(d_rank, down_first).astype(BF16)
    gates = pad_lanes(gating)

    places = [(dp + n_dp - k) % n_dp * n_wt + (wt + n_wt - b) % n_wt for k, b in order]

    def place_of(expert, row):
        return jnp.stack([x.astype(jnp.int32) for x in (seq * exp_dev + expert, row, *places)])

    chip_rows = 2 * local
    firsts = []
    for k, chip in chip_turns(n_seq):
        firsts.append(
            list(run_experts(
                place_of(0, chip * (chip_rows // TILE)), normed_m, d_out_all, gates, zbias, sbias,
                mats, None, ahead, experts_all, chip_rows, False,
            ))
        )
        if len(firsts) == 1:
            behind.advance(firsts[0][2])
    behind = behind.finish()
    turns, arrived, waiting = [], [], None
    firsts[0][2], _ = tie((firsts[0][2], firsts[-1][2]))
    for (k, chip), carried in zip(chip_turns(n_seq), firsts):
        place = place_of(split, chip * (chip_rows // TILE))
        if waiting is not None:
            place, sent = tie((place, waiting[1].astype(BF16)))
            arrived.append(shift_chip(sent, n_seq, waiting[0]))
        parts = run_experts(
            place, normed_m, d_out_all, gates, zbias, sbias, mats, carried, behind,
            experts_all, chip_rows, True,
        )
        parts = list(parts)
        if arrived:
            arrived[-1], parts[1] = tie((arrived[-1], parts[1]))
        turns.append((k, chip, parts))
        waiting = (k, core_sum(parts[1].reshape(2, local, -1), n_seq))
    back_sum = waiting[1] + sum(x.astype(F32) for x in arrived)

    upstream = cotangent[0].astype(F32)
    residual_own = own_rows(residual)
    gating_own = own_rows(gating)
    small_m_own = own_rows(small_m)
    d_gating = (
        back_sum[:, MODEL_WIDTH : MODEL_WIDTH + experts_all]
        + back_sum[:, MODEL_WIDTH + experts_all : MODEL_WIDTH + 2 * experts_all]
    )
    d_logits = gating_own * (d_gating - jnp.sum(d_gating * gating_own, axis=-1, keepdims=True))
    d_logits_low = d_logits.astype(BF16)
    d_small_m = jnp.concatenate(
        [dot_nt(d_logits_low, router_second), back_sum[:, MODEL_WIDTH + SMALL_AT :]], axis=1
    ).astype(BF16)
    small_d = back_sum[:, MODEL_WIDTH + DOWN_AT : MODEL_WIDTH + DOWN_AT + rank].astype(BF16)
    d_normed_m = back_sum[:, :MODEL_WIDTH] + dot_nt(
        jnp.concatenate([d_small_m, d_logits_low], axis=1), mix_router
    )
    d_residual = upstream + norm_backward(
        residual_own, own_rows(inverse_m), gain_second, d_normed_m
    )
    d_branch = d_residual.astype(BF16)
    d_small_o = dot_nt(d_branch, out_second).astype(BF16)
    d_att = (dot_nt(out_weight, d_branch) + dot_nt(out_first, d_small_o)).astype(BF16)
    d_att_own = d_att
    d_att = spread_seq(d_att.reshape(n_seq, q_width, local), n_seq)

    def of_chip(x, chip, axis=0):
        return lax.dynamic_slice_in_dim(x, chip * chip_rows, chip_rows, axis)

    d_small_o_late, d_branch_late, d_small_m_late, small_d_late, _ = tie(
        (d_small_o, d_branch, d_small_m, small_d, d_att_own)
    )
    grad_gu = sum(dot_tn(of_chip(small_m[:, rank:], chip), parts[4]) for _, chip, parts in turns)
    grad_down = sum(dot_tn(of_chip(d_rank, chip), parts[3]) for _, chip, parts in turns)
    att_own = lax.dynamic_slice_in_dim(att, seq * local, local, 1)
    early = jnp.concatenate(
        [
            dot(d_small_o_late, att_own, ((0,), (1,))),
            dot_tn(own_rows(small_o), d_branch_late),
            dot_tn(d_small_m_late, own_rows(normed_m)),
            dot_tn(small_d_late, cotangent[0]),
            jnp.concatenate([grad_gu[:rank, :HIDDEN], grad_gu[rank:, HIDDEN:], grad_down], axis=1),
            pad_lanes(dot_tn(small_m_own[:, :rank], d_logits_low), width=MODEL_WIDTH),
        ],
        axis=0,
    )
    early = reduce_seq(early, n_seq)
    parts_out = [core_sum(parts[0].reshape(2, local, -1), n_seq) for _, _, parts in turns]
    early, d_att, *parts_sent = tie((early, d_att, *[x.astype(BF16) for x in parts_out[:-1]]))
    early = lax.all_gather(tagged(early, index_now), ("dp", "wt"), axis=0)
    sent = [shift_chip(x, n_seq, k) for x, (k, _, _) in zip(parts_sent, turns)]
    dqt, dkt, dvt = attend_back(
        qt, kt, vt, ot, d_att.reshape(n_seq, kv_local, group, HEAD, local), probs, inverse_l,
        cosine, sine,
    )
    dqt, *sent = tie((dqt, *sent))
    output_rows = residual_own + dot(small_d, down_second) + parts_out[-1]
    output_rows = output_rows + sum(x.astype(F32) for x in sent)

    d_qkv = jnp.concatenate(
        [dqt.reshape(q_width, total), dkt.reshape(k_width, total), dvt.reshape(k_width, total)], 0
    )
    d_small_a = dot(d_qkv, second, ((0,), (1,))).astype(BF16)
    grad_second = dot(small_a, d_qkv, ((0,), (1,)))

    def spread(x, width, full):
        return lax.dynamic_update_slice_in_dim(
            jnp.zeros((x.shape[0], full), F32), x, seq * width, 1
        )

    late = jnp.concatenate(
        [
            dot_tn(d_small_a, normed),
            spread(grad_second[:rank, :q_width], q_width, MODEL_WIDTH),
            jnp.concatenate(
                [
                    spread(grad_second[rank : 2 * rank, q_width : q_width + k_width], k_width, KEY_FEATURES),
                    spread(grad_second[2 * rank :, q_width + k_width :], k_width, KEY_FEATURES),
                    jnp.zeros((rank, MODEL_WIDTH - 2 * KEY_FEATURES), F32),
                ],
                axis=1,
            ),
        ],
        axis=0,
    )
    late = reduce_seq(late, n_seq)
    d_normed = None
    for k, chip in chip_turns(n_seq):
        part = dot(of_chip(d_qkv, chip, 1), qkv_weight, ((0,), (1,)))
        part = part + dot_nt(of_chip(d_small_a, chip), attn_first)
        part = core_sum(part.astype(BF16).reshape(2, local, MODEL_WIDTH), n_seq)
        if k:
            late, part = tie((late, part.astype(BF16)))
            part = shift_chip(part, n_seq, k).astype(F32)
        d_normed = part if d_normed is None else d_normed + part
    input_grad = d_residual + norm_backward(
        tokens[0].astype(F32), own_rows(inverse_a), gain_first, d_normed
    )
    names = early[:, -1, 0].astype(jnp.int32)
    early = by_adapter(early[:, :-8], names, n_seq, n_wt)
    turned = jnp.stack(
        [
            (dp + n_dp - k) % n_dp * n_wt + (wt + n_wt - b) % n_wt
            for b in range(n_wt) for k in range(n_dp)
        ]
    )
    late = by_adapter(gather_groups(late.astype(BF16), n_dp, n_wt), names[turned], n_seq, n_wt)

    def flip(x):
        return jnp.swapaxes(x, 1, 2)

    def at(flat, row, count, lo=0, hi=MODEL_WIDTH):
        return flat[:, row : row + count, lo:hi]

    low = 6 * rank
    return (
        output_rows[None].astype(BF16),
        input_grad[None],
        flip(at(late, 0, 3 * rank)),
        at(late, 3 * rank, rank),
        jnp.stack(
            [at(late, 4 * rank, rank, m, m + KEY_FEATURES) for m in (0, KEY_FEATURES)], axis=1
        ),
        flip(at(early, 0, rank)),
        at(early, rank, rank),
        flip(at(early, 2 * rank, 3 * rank)),
        at(early, low + rank, rank, 0, experts_all),
        jnp.stack([at(early, low, rank, m, m + HIDDEN) for m in (0, HIDDEN)], axis=1),
        flip(at(early, low, rank, 2 * HIDDEN, 3 * HIDDEN)),
        at(early, 5 * rank, rank),
    )


def solution(mesh):
    split = P(("dp", "wt"), "seq", None)
    rows = P(("dp", "wt"), None)
    bank = P("wt", None, None)
    placed = (
        split, split, split, rows, P(("dp", "wt")), P(), rows, rows, rows, P(), rows,
        P("seq", ("dp", "wt"), None), P("seq", ("dp", "wt"), None),
    ) + (P(),) * 10
    wide = P("wt", None, None, None)
    return jax.shard_map(
        shards,
        mesh=mesh,
        in_specs=placed,
        out_specs=(split, split, bank, bank, wide, bank, bank, bank, bank, wide, bank, bank),
        check_vma=False,
    )
```
